512 devices in a mesh: rep: 8 (over z), fsdp: 64 (over y, x, core).
Axes of the slice: x: 4, y: 8, z: 8, core: 2. Of those that a mesh axis runs over, the one named last changes fastest.
Arguments:
- grads: bfloat16 [8, 2, 1024, 8192], P('rep', None, 'fsdp'), may hold values from -6 to 6
- params: bfloat16 [2, 1024, 8192], P(None, 'fsdp', 'rep'), may hold values from -6 to 6
- left_basis: bfloat16 [2, 1024, 1024], P(None, 'fsdp'), may hold values from -0.1875 to 0.1875
- right_basis: bfloat16 [2, 8192, 1024], P(None, ('rep', 'fsdp')), may hold values from -0.1875 to 0.1875
- moment: float32 [2, 1024, 8192], P(None, 'fsdp', 'rep'), may hold values from -6 to 6
- codes: int32 [2, 1024, 8192], P(None, 'fsdp', 'rep'), may hold values from 0 to 15, as said below
- level_low: float32 [2, 64], P(None, 'rep'), may hold values from 0.2 to 2
- level_span: float32 [2, 64], P(None, 'rep'), may hold values from 0.5 to 8
Outputs:
- params_new: bfloat16 [2, 1024, 8192], P(None, 'fsdp')
- moment_new: float32 [2, 1024, 8192], P(None, 'fsdp', 'rep')
- update: float32 [2, 1024, 8192], P(None, 'fsdp', 'rep')
- levels: float32 [2, 1024, 8192], P(None, 'fsdp', 'rep')
- low_new: float32 [2, 64], P(None, 'rep')
- span_new: float32 [2, 64], P(None, 'rep')
The draws below stay inside these ranges and needn't reach their ends.
Inputs may be any that keep to these rules, and one draw needn't show every extreme that they name: `codes`: in each layer and quantization group exactly one entry has code 0; all others are 1 to 15.
All inputs are finite; a program needn't handle non-finite values.
Results may differ from the reference program's by a relative error of at most 0.017.
Values may be sent and summed in bfloat16 or wider, within the bound.
No kernel may reach another device: no remote copies, remote signals or barrier semaphores. Data moves between devices by JAX's collectives and lax.ppermute only.
A program may use at most 64 MiB of HBM per device.

```python
import math
import jax
import jax.numpy as jnp
from jax import lax

LAYERS = 2
BLOCK = 1024
QGROUP = 128
REPLICAS = 8
COLS = 8192
GROUPS = 64
N_REP = 8


def draw_codes(key, part):
    key = jax.random.fold_in(key, 7)
    base_key, spot_key = jax.random.split(key)
    base_codes = jax.random.randint(base_key, (LAYERS, BLOCK, COLS), 1, 16, dtype=jnp.int32)
    chosen = jax.random.randint(spot_key, (LAYERS, GROUPS), 0, BLOCK * QGROUP, dtype=jnp.int32)
    row_index = jnp.arange(BLOCK, dtype=jnp.int32)[:, None]
    col_index = jnp.arange(COLS, dtype=jnp.int32)[None, :]
    within = row_index * QGROUP + col_index % QGROUP
    group_of = jnp.arange(COLS, dtype=jnp.int32) // QGROUP
    target = chosen[:, group_of][:, None, :]
    return jnp.where(within[None, :, :] == target, jnp.int32(0), base_codes)


def strengthened(values, own_key, source, target, shards_of, factor):
    owner, partner = [(jnp.arange(values.shape[dim]) // (values.shape[dim] // shards_of)).reshape([-1 if axis == dim else 1 for axis in range(values.ndim)]) for dim in (source, target)]
    chosen = jax.random.permutation(own_key, shards_of)[partner]
    strong = (owner == chosen) | (owner == (partner + shards_of // 2) % shards_of)
    return jnp.where(strong, factor * values, values)


def level_of(stream_key, dims, pieces, low, largest):
    gain, own = 1.0, jax.random.fold_in(stream_key, 6)
    for position, shards_of in pieces:
        steps = jnp.exp(jax.random.uniform(jax.random.fold_in(own, position), (shards_of,), jnp.float32, low / len(pieces), largest / len(pieces)))
        gain = gain * jnp.repeat(steps, dims[position] // shards_of).reshape([-1 if axis == position else 1 for axis in range(len(dims))])
    return gain


def noise(stream_key, extent, spread, limit, cuts=(), kind=jnp.bfloat16):
    drawn = jax.random.normal(stream_key, extent, jnp.float32) * spread
    if len(cuts) > 0:
        drawn = level_of(stream_key, extent, cuts, -0.22, 0.18) * drawn
    return jnp.clip(drawn, min=-limit, max=limit).astype(kind)


def bell_draw_with(stream_key, dims, width, limit, cuts, heavy, held_as=jnp.bfloat16):
    entries = width * jax.random.normal(stream_key, dims, jnp.float32)
    if cuts:
        entries = entries * level_of(stream_key, dims, cuts, -0.22, 0.18)
    return jnp.clip(strengthened(entries, jax.random.fold_in(stream_key, 3), *heavy), -limit, limit).astype(held_as)


def setup_inputs(seed: int = 0) -> dict:
    streams_of = jax.random.split(jax.random.key(seed), 9)
    grads = bell_draw_with(streams_of[0], (REPLICAS, LAYERS, BLOCK, COLS), 1.0, 6.0, ((0, 8), (2, 64)), (0, 3, 8, 2.0))
    params = noise(streams_of[1], (LAYERS, BLOCK, COLS), 1.0, 6.0, ((1, 64), (2, 8)))
    left_basis = noise(streams_of[2], (LAYERS, BLOCK, BLOCK), BLOCK ** -0.5, 0.1875, ((1, 64),))
    right_basis = noise(streams_of[3], (LAYERS, COLS, BLOCK), BLOCK ** -0.5, 0.1875, ((1, 512),))
    moment = noise(streams_of[4], (LAYERS, BLOCK, COLS), 1.0, 6.0, ((1, 64), (2, 8)), jnp.float32)
    codes = draw_codes(jax.random.fold_in(streams_of[8], 71), 0)
    level_low = jnp.clip(jnp.exp(math.log(2.0) - 2.3025851 * jax.random.uniform(streams_of[6], (LAYERS, GROUPS), jnp.float32) ** level_of(streams_of[6], (LAYERS, GROUPS), ((1, 8),), -0.2, 0.2)), 0.2, 2.0)
    level_span = jnp.clip(jnp.exp(math.log(8.0) - 2.7725887 * jax.random.uniform(streams_of[7], (LAYERS, GROUPS), jnp.float32) ** level_of(streams_of[7], (LAYERS, GROUPS), ((1, 8),), -0.2, 0.2)), 0.5, 8.0)
    return dict(grads=grads, params=params, left_basis=left_basis, right_basis=right_basis, moment=moment, codes=codes, level_low=level_low, level_span=level_span)


def reference(grads, params, left_basis, right_basis, moment, codes, level_low, level_span):
    summed = lax.optimization_barrier(jnp.sum(grads.astype(jnp.float32), axis=0))
    grad16 = summed.astype(jnp.bfloat16)
    right_blocks = right_basis.reshape(LAYERS, N_REP, BLOCK, BLOCK).astype(jnp.float32)
    left_whole = left_basis.astype(jnp.float32)
    grad_blocks = grad16.reshape(LAYERS, BLOCK, N_REP, BLOCK).astype(jnp.float32)
    projected = jnp.einsum('lirk,lrkj->lirj', grad_blocks, right_blocks).astype(jnp.bfloat16)
    rotated = jnp.einsum('lki,lkrj->lirj', left_whole, projected.astype(jnp.float32))
    rotated = rotated.reshape(LAYERS, BLOCK, COLS)
    moment_new = 0.9 * moment + 0.1 * rotated
    low_wide = jnp.repeat(level_low, QGROUP, axis=1)[:, None, :]
    span_wide = jnp.repeat(level_span, QGROUP, axis=1)[:, None, :]
    second = low_wide + codes.astype(jnp.float32) / 15.0 * span_wide
    second_new = 0.95 * second + 0.05 * rotated * rotated
    scaled = (moment_new / (jnp.sqrt(second_new) + 1e-08)).astype(jnp.bfloat16)
    scaled_blocks = scaled.reshape(LAYERS, BLOCK, N_REP, BLOCK).astype(jnp.float32)
    returned = jnp.einsum('lirk,lrjk->lirj', scaled_blocks, right_blocks).astype(jnp.bfloat16)
    update = jnp.einsum('lik,lkrj->lirj', left_whole, returned.astype(jnp.float32))
    update = update.reshape(LAYERS, BLOCK, COLS)
    params_new = (params.astype(jnp.float32) * (1.0 - 0.05 * 0.1) - 0.05 * update).astype(jnp.bfloat16)
    grouped = second_new.reshape(LAYERS, BLOCK, GROUPS, QGROUP)
    low_new = lax.optimization_barrier(jnp.min(grouped, axis=(1, 3)))
    highest = lax.optimization_barrier(jnp.max(grouped, axis=(1, 3)))
    span_new = highest - low_new
    levels = 15.0 * (grouped - low_new[:, None, :, None]) / span_new[:, None, :, None]
    levels = levels.reshape(LAYERS, BLOCK, COLS)
    return (params_new, moment_new, update, levels, low_new, span_new)
```

```python
import jax
import jax.numpy as jnp
from jax import lax
from jax.sharding import Mesh, PartitionSpec as P

QGROUP = 128
F = ("y", "x", "core")
ZQ = ("rep", "x", "core")
Q = ("x", "core")


def exchange(blocks, axes):
    return lax.all_to_all(blocks, axes, split_axis=0, concat_axis=0, tiled=True)


def pieces(values):
    first = lax.reduce_precision(values, 8, 7)
    rest = values - first
    second = lax.reduce_precision(rest, 8, 7)
    third = rest - second
    return jnp.stack([first, second, third]).astype(jnp.bfloat16)


def on_device(grads, params, left_basis, right_basis, moment, codes, level_low, level_span):
    bf16, f32 = jnp.bfloat16, jnp.float32
    both = jnp.broadcast_to(right_basis[None, None], (4, 2, 2, 16, 1024))
    lefts = jnp.broadcast_to(left_basis[None, :, None], (4, 2, 1, 16, 1024))
    bases = exchange(jnp.concatenate([both, lefts], axis=2).reshape(8, 3, 16, 1024), Q)
    right_y = bases[:, :2].transpose(1, 0, 2, 3).reshape(2, 128, 1024)
    left_y = bases[:, 2].reshape(128, 1024)
    right = lax.all_gather(right_y, "y", axis=1, tiled=True)

    sent = grads[0].reshape(2, 16, 8, 4, 256).transpose(2, 3, 0, 1, 4).reshape(64, 16, 256)
    got = exchange(sent, ZQ).reshape(8, 128, 256)
    grad16 = jnp.sum(got.astype(f32), axis=0).astype(bf16)
    part = jnp.einsum("ki,kj->ij", left_y, grad16, preferred_element_type=f32).astype(bf16)
    got = exchange(part.reshape(64, 16, 256), F).reshape(8, 4, 2, 16, 256)
    turned = jnp.sum(got.astype(f32), axis=0).transpose(1, 2, 0, 3).reshape(2, 16, 1024).astype(bf16)

    doubled = jnp.concatenate([params, jnp.zeros_like(params)], axis=0)
    params_all = lax.all_gather(doubled, "rep", axis=0)[:, :2]

    rotated = jnp.einsum("lik,lkj->lij", turned, right, preferred_element_type=f32)
    moment_new = 0.9 * moment + 0.1 * rotated
    grouped = rotated.reshape(2, 16, 8, QGROUP)
    code_grouped = codes.reshape(2, 16, 8, QGROUP).astype(f32)
    second = level_low[:, None, :, None] + code_grouped / 15.0 * level_span[:, None, :, None]
    second_new = 0.95 * second + 0.05 * grouped * grouped
    flat = second_new.reshape(2, 16, 1024)
    scaled = (moment_new / (jnp.sqrt(flat) + 1e-08)).astype(bf16)
    returned = jnp.einsum("lik,ljk->lij", scaled, right, preferred_element_type=f32).astype(bf16)

    ends = jnp.stack([jnp.min(second_new, axis=(1, 3)), jnp.max(second_new, axis=(1, 3))])
    row = jnp.pad(pieces(ends).reshape(1, 96), ((0, 7), (0, 32)))
    block = returned.reshape(2, 16, 4, 2, 128).transpose(2, 0, 3, 1, 4).reshape(4, 2, 32, 128)
    block = jnp.concatenate([block, jnp.broadcast_to(row, (4, 2, 8, 128))], axis=2)
    got = exchange(jnp.broadcast_to(block[None], (8, 4, 2, 40, 128)).reshape(64, 40, 128), F)
    back = got[:, :32].reshape(64, 2, 16, 128).transpose(0, 2, 1, 3).reshape(1024, 256)
    ends = got[:, 32, :96].astype(f32).reshape(64, 3, 2, 2, 8)
    ends = (ends[:, 0] + ends[:, 1]) + ends[:, 2]
    low_new = jnp.min(ends[:, 0], axis=0)
    span_new = jnp.max(ends[:, 1], axis=0) - low_new

    moved = jnp.einsum("ki,ij->kj", left_y, back, preferred_element_type=f32).astype(bf16)
    moved = jnp.broadcast_to(moved.reshape(1, 8, 16, 256), (8, 8, 16, 256)).reshape(64, 16, 256)
    got = exchange(moved, ZQ).reshape(8, 4, 2, 16, 256)

    levels = 15.0 * (second_new - low_new[:, None, :, None]) / span_new[:, None, :, None]
    levels = levels.reshape(2, 16, 1024)
    mine = lax.dynamic_index_in_dim(got, lax.axis_index("rep"), 0, keepdims=False)
    update = mine.transpose(1, 2, 0, 3).reshape(2, 16, 1024).astype(f32)
    every = got.transpose(2, 3, 0, 1, 4).reshape(2, 16, 8192).astype(f32)
    old = params_all.transpose(1, 2, 0, 3).reshape(2, 16, 8192).astype(f32)
    params_new = (old * (1.0 - 0.05 * 0.1) - 0.05 * every).astype(bf16)
    return (params_new, moment_new, update, levels, low_new, span_new)


def solution(mesh):
    fine = Mesh(mesh.devices.reshape(8, 8, 4, 2), ("rep", "y", "x", "core"))
    return jax.shard_map(
        on_device,
        mesh=fine,
        in_specs=(
            P("rep", None, F, None),
            P(None, F, "rep"),
            P(None, F, None),
            P(None, ("rep",) + F, None),
            P(None, F, "rep"),
            P(None, F, "rep"),
            P(None, "rep"),
            P(None, "rep"),
        ),
        out_specs=(
            P(None, F, None),
            P(None, F, "rep"),
            P(None, F, "rep"),
            P(None, F, "rep"),
            P(None, "rep"),
            P(None, "rep"),
        ),
        check_vma=False,
    )
```

```python
import jax
import jax.numpy as jnp
from jax import lax
from jax.sharding import Mesh, PartitionSpec as P

QGROUP = 128
F = ("y", "x", "core")
ZQ = ("rep", "x", "core")
Q = ("x", "core")
YX = ("y", "x")


def exchange(blocks, axes):
    return lax.all_to_all(blocks, axes, split_axis=0, concat_axis=0, tiled=True)


def shift(block, axis, size, by):
    return lax.ppermute(block, axis, [(i, (i + by) % size) for i in range(size)])


def around(block, axis):
    up, down = [block], [block]
    for _ in range(3):
        up.append(shift(up[-1], axis, 8, 1))
        down.append(shift(down[-1], axis, 8, -1))
    up.append(shift(up[-1], axis, 8, 1))
    return up + down[:0:-1]


def pieces(values):
    first = lax.reduce_precision(values, 8, 7)
    rest = values - first
    second = lax.reduce_precision(rest, 8, 7)
    third = rest - second
    return jnp.stack([first, second, third]).astype(jnp.bfloat16)


def on_device(grads, params, left_basis, right_basis, moment, codes, level_low, level_span):
    bf16, f32 = jnp.bfloat16, jnp.float32
    core = lax.axis_index("core")
    y = lax.axis_index("y")
    pick = lambda values, at: lax.dynamic_index_in_dim(values, at, 0, keepdims=False)

    def own_layer(own, other):
        return jnp.where(core == 0, jnp.concatenate([own, other], -2), jnp.concatenate([other, own], -2))

    bases = jnp.stack([right_basis, left_basis], axis=1)
    bases = jnp.broadcast_to(bases[None], (4, 2, 2, 16, 1024)).reshape(8, 2, 16, 1024)
    bases = exchange(bases, Q)
    right_y = bases[:, 0].reshape(128, 1024)
    left_y = bases[:, 1].reshape(128, 1024)

    sent = grads[0].reshape(2, 16, 8, 4, 256).transpose(2, 3, 0, 1, 4).reshape(64, 16, 256)
    got = exchange(sent, ZQ).reshape(8, 128, 256)
    grad16 = jnp.sum(got.astype(f32), axis=0).astype(bf16)
    part = jnp.einsum("ki,kj->ij", left_y, grad16, preferred_element_type=f32).astype(bf16)

    right = jnp.concatenate(around(right_y, "y"), axis=0)
    state = jnp.stack([moment, codes.astype(f32)], axis=1)
    state = own_layer(pick(state, core), shift(pick(state, 1 - core), "core", 2, 1))

    got = exchange(part.reshape(32, 32, 256), YX).reshape(8, 4, 32, 256)
    turned = jnp.sum(got.astype(f32), axis=0).transpose(1, 0, 2).reshape(32, 8, 128).astype(bf16)
    order = jnp.mod(y - jnp.arange(8), 8)
    turned = jnp.take(turned, order, axis=1).reshape(32, 1024)

    rotated = jnp.einsum("ik,kj->ij", turned, right, preferred_element_type=f32)
    low, span = pick(level_low, core), pick(level_span, core)

    def second_of(code_values, rotated, low, span):
        second = low[..., None, :, None] + code_values / 15.0 * span[..., None, :, None]
        return 0.95 * second + 0.05 * rotated * rotated

    second_new = second_of(state[1].reshape(32, 8, QGROUP), rotated.reshape(32, 8, QGROUP), low, span)
    moment_mid = 0.9 * state[0] + 0.1 * rotated
    scaled = (moment_mid / (jnp.sqrt(second_new.reshape(32, 1024)) + 1e-08)).astype(bf16)
    returned = jnp.einsum("ik,jk->ij", scaled, right, preferred_element_type=f32).astype(bf16)
    returned = jnp.take(returned.reshape(32, 8, 128), order, axis=1)

    ends = jnp.stack([jnp.min(second_new, axis=(0, 2)), jnp.max(second_new, axis=(0, 2))])
    row = jnp.pad(pieces(ends).reshape(1, 48), ((0, 7), (0, 80)))
    block = returned.reshape(32, 4, 2, 128).transpose(1, 2, 0, 3).reshape(4, 64, 128)
    block = jnp.concatenate([block, jnp.broadcast_to(row, (4, 8, 128))], axis=1)
    got = exchange(jnp.broadcast_to(block[None], (8, 4, 72, 128)).reshape(32, 72, 128), YX)
    back = got[:, :64].reshape(32, 2, 32, 128).transpose(0, 2, 1, 3).reshape(1024, 256)
    ends = got[:, 64, :48].astype(f32).reshape(32, 3, 2, 8)
    ends = (ends[:, 0] + ends[:, 1]) + ends[:, 2]
    ends = jnp.stack([jnp.min(ends[:, 0], axis=0), jnp.max(ends[:, 1], axis=0)])

    moved = jnp.einsum("ki,ij->kj", left_y, back, preferred_element_type=f32).astype(bf16)
    moved = jnp.broadcast_to(moved.reshape(1, 8, 16, 256), (8, 8, 16, 256)).reshape(64, 16, 256)
    got = exchange(moved, ZQ).reshape(8, 4, 2, 16, 256)

    rotated = rotated.reshape(2, 16, 1024)
    here, there = pick(rotated, core), shift(pick(rotated, 1 - core), "core", 2, 1)
    both = lambda here, there: jnp.where(core == 0, jnp.stack([here, there]), jnp.stack([there, here]))
    rotated = both(here, there)
    ends = both(ends, shift(ends, "core", 2, 1))
    low_new = ends[:, 0]
    span_new = ends[:, 1] - low_new
    moment_new = 0.9 * moment + 0.1 * rotated
    second_new = second_of(
        codes.astype(f32).reshape(2, 16, 8, QGROUP), rotated.reshape(2, 16, 8, QGROUP), level_low, level_span
    )
    levels = 15.0 * (second_new - low_new[:, None, :, None]) / span_new[:, None, :, None]
    levels = levels.reshape(2, 16, 1024)

    rep = lax.axis_index("rep")
    update = pick(got, rep).transpose(1, 2, 0, 3).reshape(2, 16, 1024).astype(f32)
    every = got.transpose(2, 3, 0, 1, 4).reshape(2, 16, 8192).astype(f32)
    olds = jnp.take(jnp.stack(around(params, "rep")), jnp.mod(rep - jnp.arange(8), 8), axis=0)
    old = olds.transpose(1, 2, 0, 3).reshape(2, 16, 8192).astype(f32)
    params_new = (old * (1.0 - 0.05 * 0.1) - 0.05 * every).astype(bf16)
    return (params_new, moment_new, update, levels, low_new, span_new)


def solution(mesh):
    fine = Mesh(mesh.devices.reshape(8, 8, 4, 2), ("rep", "y", "x", "core"))
    return jax.shard_map(
        on_device,
        mesh=fine,
        in_specs=(
            P("rep", None, F, None),
            P(None, F, "rep"),
            P(None, F, None),
            P(None, ("rep",) + F, None),
            P(None, F, "rep"),
            P(None, F, "rep"),
            P(None, "rep"),
            P(None, "rep"),
        ),
        out_specs=(
            P(None, F, None),
            P(None, F, "rep"),
            P(None, F, "rep"),
            P(None, F, "rep"),
            P(None, "rep"),
            P(None, "rep"),
        ),
        check_vma=False,
    )
```

```python
import jax
import jax.numpy as jnp
from jax import lax
from jax.experimental import pallas as pl
from jax.experimental.pallas import tpu as pltpu
from jax.sharding import Mesh, PartitionSpec as P

QGROUP = 128
F = ("y", "x", "core")
ZQ = ("rep", "x", "core")
Q = ("x", "core")
YX = ("y", "x")
BF16, F32 = jnp.bfloat16, jnp.float32
VMEM = pl.BlockSpec(memory_space=pltpu.VMEM)
SMEM = pl.BlockSpec(memory_space=pltpu.SMEM)
ANY = pl.BlockSpec(memory_space=pl.ANY)


def shape(*dims, of=BF16):
    return jax.ShapeDtypeStruct(dims, of)


def exchange(blocks, axes):
    return lax.all_to_all(blocks, axes, split_axis=0, concat_axis=0, tiled=True)


def shift(block, axis, size, by):
    return lax.ppermute(block, axis, [(i, (i + by) % size) for i in range(size)])


def bases_kernel(right, left, out):
    for panel in range(4):
        out[panel, :, 0] = right[...]
        out[panel, :, 1] = left[...]


def bases_out(right, left):
    return pl.pallas_call(
        bases_kernel, out_shape=shape(4, 2, 2, 16, 1024), in_specs=[VMEM, VMEM], out_specs=VMEM
    )(right, left)


def panels_kernel(grads, out):
    for panel in range(32):
        out[panel] = grads[:, :, panel * 256 : panel * 256 + 256]


def panels(grads):
    return pl.pallas_call(
        panels_kernel, out_shape=shape(32, 2, 16, 256), in_specs=[VMEM], out_specs=VMEM
    )(grads)


def left_kernel(grads, left, out):
    total = grads[0].astype(F32)
    for replica in range(1, 8):
        total += grads[replica].astype(F32)
    part = lax.dot_general(
        left[...], total.astype(BF16), (((0,), (0,)), ((), ())), preferred_element_type=F32
    )
    out[...] = part.astype(BF16)


def left_part(grads, left):
    return pl.pallas_call(
        left_kernel, out_shape=shape(1024, 256), in_specs=[VMEM, VMEM], out_specs=VMEM
    )(grads, left)


def middle_kernel(
    got, own, far, up, down, more, moment, codes, state, low, span, out, mine, others, right, rotated, scaled, sems
):
    core, at = lax.axis_index("core"), lax.axis_index("y")
    ring = [own, up.at[0], more.at[0], down.at[1], far, up.at[1], more.at[1], down.at[0]]
    copies = []
    for back, block in enumerate(ring):
        place = lax.rem(at + 8 - back, 8)
        copies.append(pltpu.make_async_copy(block, right.at[place], sems.at[back]))
    for copy in copies:
        copy.start()
    turned = []
    for panel in range(4):
        total = got[0, panel].astype(F32)
        for part in range(1, 8):
            total += got[part, panel].astype(F32)
        turned.append(total.astype(BF16))
    turned = jnp.concatenate(turned, axis=1)
    for copy in copies:
        copy.wait()
    basis = right[...].reshape(1024, 1024)
    rotated[...] = jnp.dot(turned, basis, preferred_element_type=F32)
    here = pl.ds(pl.multiple_of(core * 16, 16), 16)
    there = pl.ds(pl.multiple_of((1 - core) * 16, 16), 16)
    mine[...] = rotated[here, :]
    others[...] = rotated[there, :]
    lows, highs = [], []
    for group in range(8):
        lanes = slice(group * 128, group * 128 + 128)
        base, width = low[core, group], span[core, group]
        ends = []
        for rows, mean, code in (
            (here, moment[core, :, lanes], codes[core, :, lanes].astype(F32)),
            (there, state[0, :, lanes], state[1, :, lanes]),
        ):
            turn = rotated[rows, lanes]
            second = 0.95 * (base + code / 15.0 * width) + 0.05 * turn * turn
            mean = 0.9 * mean + 0.1 * turn
            scaled[rows, lanes] = mean / (jnp.sqrt(second) + 1e-08)
            ends.append(second)
        lows.append(jnp.min(jnp.minimum(*ends), axis=0, keepdims=True))
        highs.append(jnp.max(jnp.maximum(*ends), axis=0, keepdims=True))
    returned = lax.dot_general(
        scaled[...].astype(BF16), basis, (((1,), (1,)), ((), ())), preferred_element_type=F32
    ).astype(BF16)
    ends = jnp.concatenate(
        [
            jnp.min(jnp.concatenate(lows, axis=0), axis=1, keepdims=True),
            jnp.max(jnp.concatenate(highs, axis=0), axis=1, keepdims=True),
        ],
        axis=0,
    )
    first = ends.astype(BF16).astype(F32)
    second = (ends - first).astype(BF16).astype(F32)
    third = ends - first - second
    lane = lax.broadcasted_iota(jnp.int32, (16, 128), 1)
    tile = jnp.where(lane == 0, first, jnp.where(lane == 1, second, jnp.where(lane == 2, third, 0.0)))
    tile = tile.astype(BF16)
    for panel in range(4):
        start = panel * 256
        for copy in range(8):
            out[copy, panel, 0:32] = returned[:, start : start + 128]
            out[copy, panel, 32:64] = returned[:, start + 128 : start + 256]
            out[copy, panel, 64:80] = tile


def middle(got, own, far, up, down, more, moment, codes, state, low, span):
    return pl.pallas_call(
        middle_kernel,
        out_shape=(shape(8, 4, 80, 128), shape(16, 1024, of=F32), shape(16, 1024, of=F32)),
        in_specs=[VMEM] + [ANY] * 5 + [VMEM] * 3 + [SMEM] * 2,
        out_specs=(VMEM, VMEM, VMEM),
        scratch_shapes=[
            pltpu.VMEM((8, 128, 1024), BF16),
            pltpu.VMEM((32, 1024), F32),
            pltpu.VMEM((32, 1024), F32),
            pltpu.SemaphoreType.DMA((8,)),
        ],
        compiler_params=pltpu.CompilerParams(vmem_limit_bytes=32 * 1024 * 1024),
    )(got, own, far, up, down, more, moment, codes, state, low, span)


def update_kernel(got, left, out, ends):
    halves = [
        jnp.dot(left[...], got[:, at : at + 32, :].reshape(1024, 128), preferred_element_type=F32)
        for at in (0, 32)
    ]
    moved = jnp.concatenate(halves, axis=1).astype(BF16).reshape(8, 16, 256)
    for copy in range(8):
        out[copy] = moved
    values = jnp.sum(got[:, 64:80, :].astype(F32), axis=2, keepdims=True)
    ends[0] = jnp.broadcast_to(jnp.min(values[:, 0:8], axis=0), (8, 128))
    ends[1] = jnp.broadcast_to(jnp.max(values[:, 8:16], axis=0), (8, 128))


def update_part(got, left):
    return pl.pallas_call(
        update_kernel,
        out_shape=(shape(8, 8, 16, 256), shape(2, 8, 128, of=F32)),
        in_specs=[VMEM, VMEM],
        out_specs=(VMEM, VMEM),
    )(got, left)


def step_kernel(got, olds, params_new, update):
    rep = lax.axis_index("rep")
    for panel in range(4):
        lanes = slice(panel * 256, panel * 256 + 256)
        update[:, :, lanes] = got[rep, panel].astype(F32)
        for block in range(8):
            change = got[block, panel].astype(F32)
            old = olds[block, :, :, lanes].astype(F32)
            new = old * (1.0 - 0.05 * 0.1) - 0.05 * change
            start = block * 1024 + panel * 256
            params_new[:, :, start : start + 256] = new.astype(BF16)


def step(got, olds):
    return pl.pallas_call(
        step_kernel,
        out_shape=(shape(2, 16, 8192), shape(2, 16, 1024, of=F32)),
        in_specs=[VMEM, VMEM],
        out_specs=(VMEM, VMEM),
    )(got, olds)


def on_device(grads, params, left_basis, right_basis, moment, codes, level_low, level_span):
    core, rep = lax.axis_index("core"), lax.axis_index("rep")
    pick = lambda values, at: lax.dynamic_index_in_dim(values, at, 0, keepdims=False)
    both = lambda here, there: jnp.where(core == 0, jnp.stack([here, there]), jnp.stack([there, here]))
    swap = lambda values: shift(values, "core", 2, 1)

    def wait(value, after):
        return lax.optimization_barrier((value, after))[0]

    bases = exchange(bases_out(right_basis, left_basis).reshape(8, 2, 16, 1024), Q)
    right_y = bases[:, 0].reshape(128, 1024)
    left_y = bases[:, 1].reshape(128, 1024)

    sent = panels(grads[0])
    got = exchange(sent.reshape(64, 16, 256), ZQ)
    part = left_part(got.reshape(8, 128, 256), left_y)

    far = shift(right_y, "y", 8, 4)
    pair = jnp.stack([right_y, far])
    up, down = shift(pair, "y", 8, 1), shift(pair, "y", 8, -1)
    more = shift(up, "y", 8, 1)

    state = jnp.stack([pick(moment, 1 - core), pick(codes, 1 - core).astype(F32)])
    state = swap(wait(state, part))

    got = exchange(part.reshape(32, 32, 256), YX).reshape(8, 4, 32, 256)
    block, mine, others = middle(
        got, right_y, far, up, down, more, moment, codes, state, level_low, level_span
    )
    got = exchange(block.reshape(32, 80, 128), YX)
    moved, ends = update_part(got, left_y)
    got = exchange(moved.reshape(64, 16, 256), ZQ).reshape(8, 4, 2, 16, 256)

    rotated = both(mine, swap(others))
    ends = ends[:, :, 0]
    ends = both(ends, swap(ends))
    low_new = ends[:, 0]
    span_new = ends[:, 1] - low_new
    moment_new = 0.9 * moment + 0.1 * rotated
    grouped = rotated.reshape(2, 16, 8, QGROUP)
    code_grouped = codes.reshape(2, 16, 8, QGROUP).astype(F32)
    second = level_low[:, None, :, None] + code_grouped / 15.0 * level_span[:, None, :, None]
    second_new = 0.95 * second + 0.05 * grouped * grouped
    levels = 15.0 * (second_new - low_new[:, None, :, None]) / span_new[:, None, :, None]
    levels = levels.reshape(2, 16, 1024)

    olds = params[None]
    for bit, start, end in ((1, sent, part), (2, part, block), (4, block, moved)):
        other = lax.ppermute(wait(olds, start), "rep", [(i, i ^ bit) for i in range(8)])
        olds, other = wait((olds, other), end)
        olds = jnp.where(rep & bit == 0, jnp.concatenate([olds, other]), jnp.concatenate([other, olds]))
    params_new, update = step(got, olds)
    return (params_new, moment_new, update, levels, low_new, span_new)


def solution(mesh):
    fine = Mesh(mesh.devices.reshape(8, 8, 4, 2), ("rep", "y", "x", "core"))
    return jax.shard_map(
        on_device,
        mesh=fine,
        in_specs=(
            P("rep", None, F, None),
            P(None, F, "rep"),
            P(None, F, None),
            P(None, ("rep",) + F, None),
            P(None, F, "rep"),
            P(None, F, "rep"),
            P(None, "rep"),
            P(None, "rep"),
        ),
        out_specs=(
            P(None, F, None),
            P(None, F, "rep"),
            P(None, F, "rep"),
            P(None, F, "rep"),
            P(None, "rep"),
            P(None, "rep"),
        ),
        check_vma=False,
    )
```

```python
import jax
import jax.numpy as jnp
from jax import lax
from jax.experimental import pallas as pl
from jax.experimental.pallas import tpu as pltpu
from jax.sharding import Mesh, PartitionSpec as P

F = ("y", "x", "core")
ZQ = ("rep", "x", "core")
Q = ("x", "core")
BF16, F32 = jnp.bfloat16, jnp.float32
VMEM = pl.BlockSpec(memory_space=pltpu.VMEM)
SMEM = pl.BlockSpec(memory_space=pltpu.SMEM)
ANY = pl.BlockSpec(memory_space=pl.ANY)
PARAMS = pltpu.CompilerParams(vmem_limit_bytes=32 * 1024 * 1024)


def shape(*dims, of=BF16):
    return jax.ShapeDtypeStruct(dims, of)


def exchange(blocks, axes):
    return lax.all_to_all(blocks, axes, split_axis=0, concat_axis=0, tiled=True)


def shift(block, axis, size, by):
    return lax.ppermute(block, axis, [(i, (i + by) % size) for i in range(size)])


def pull(refs, places, sems):
    copies = [
        pltpu.make_async_copy(ref, place, sems.at[i])
        for i, (ref, place) in enumerate(zip(refs, places))
    ]
    for copy in copies:
        copy.start()

    def wait():
        for copy in copies:
            copy.wait()

    return wait


def quarters(tiles, lane):
    turned = []
    for to in range(4):
        new = None
        for part in range(4):
            tile = tiles[part]
            by = (32 * (part - to)) % 128
            tile = pltpu.roll(tile, by, 1) if by else tile
            new = tile if new is None else jnp.where(lane >= 32 * part, tile, new)
        turned.append(new)
    return turned


def panels_kernel(grads, left, out):
    lane = lax.broadcasted_iota(jnp.int32, (32, 128), 1)
    eighth = pl.ds(pl.multiple_of(lax.axis_index("rep") * 128, 128), 128)
    basis = left[:, :, eighth]
    for block in range(8):
        for half in range(2):
            start = block * 1024 + half * 512
            tiles = [
                grads[:, :, start + 128 * i : start + 128 * i + 128].astype(F32).reshape(32, 128)
                for i in range(4)
            ]
            for x, tile in enumerate(quarters(tiles, lane)):
                out[block, x, :, :, half * 128 : half * 128 + 128] = tile.astype(BF16).reshape(2, 16, 128)
        for x in range(4):
            out[block, x, :, :, 256:384] = basis


def panels(grads, left):
    return pl.pallas_call(
        panels_kernel, out_shape=shape(8, 4, 2, 16, 384), in_specs=[VMEM, VMEM], out_specs=VMEM
    )(grads, left)


def left_kernel(grads, out, left, held, sems):
    wait = pull([grads], [held], sems)
    wait()
    total = held[0, :, 0:256].astype(F32)
    for replica in range(1, 8):
        total += held[replica, :, 0:256].astype(F32)
    for replica in range(8):
        left[:, replica * 128 : replica * 128 + 128] = held[replica, :, 256:384]
    part = lax.dot_general(
        left[...], total.astype(BF16), (((0,), (0,)), ((), ())), preferred_element_type=F32
    )
    out[...] = part.astype(BF16)


def left_part(grads):
    return pl.pallas_call(
        left_kernel,
        out_shape=(shape(1024, 256), shape(128, 1024)),
        in_specs=[ANY],
        out_specs=(VMEM, VMEM),
        scratch_shapes=[pltpu.VMEM((8, 128, 384), BF16), pltpu.SemaphoreType.DMA((1,))],
        compiler_params=PARAMS,
    )(grads)


def right_kernel(got, own, far, up, down, more, out, right_out, held, right, sems):
    at = lax.axis_index("y")
    ring = [own, up.at[0], more.at[0], down.at[1], far, up.at[1], more.at[1], down.at[0]]
    places = [right.at[lax.rem(at + 8 - back, 8)] for back in range(8)]
    wait = pull([got] + ring, [held] + places, sems)
    wait()
    total = held[0].astype(F32)
    for part in range(1, 8):
        total += held[part].astype(F32)
    basis = right[...].reshape(256, 1024)
    out[...] = jnp.dot(total.astype(BF16), basis, preferred_element_type=F32).astype(BF16)
    right_out[...] = basis


def right_part(got, pieces):
    return pl.pallas_call(
        right_kernel,
        out_shape=(shape(128, 1024), shape(256, 1024)),
        in_specs=[ANY] * 6,
        out_specs=(VMEM, VMEM),
        scratch_shapes=[
            pltpu.VMEM((8, 128, 256), BF16),
            pltpu.VMEM((8, 32, 1024), BF16),
            pltpu.SemaphoreType.DMA((9,)),
        ],
        compiler_params=PARAMS,
    )(got, *pieces)


def ends_tile(ends):
    first = ends.astype(BF16).astype(F32)
    second = (ends - first).astype(BF16).astype(F32)
    third = ends - first - second
    lane = lax.broadcasted_iota(jnp.int32, (16, 128), 1)
    tile = jnp.where(lane == 0, first, jnp.where(lane == 1, second, jnp.where(lane == 2, third, 0.0)))
    return tile.astype(BF16)


def ends_of(tiles):
    values = jnp.sum(tiles.astype(F32), axis=2, keepdims=True)
    return jnp.min(values[:, 0:8], axis=0), jnp.max(values[:, 8:16], axis=0)


def moments_kernel(got, moment, codes, low, span, out, moment_new, second_new, held, sems):
    wait = pull([got], [held], sems)
    wait()
    for layer in range(2):
        lows, highs = [], []
        for group in range(8):
            lanes = slice(group * 128, group * 128 + 128)
            turn = held[0, layer, :, lanes].astype(F32)
            for part in range(1, 4):
                turn += held[part, layer, :, lanes].astype(F32)
            mean = 0.9 * moment[layer, :, lanes] + 0.1 * turn
            code = codes[layer, :, lanes].astype(F32)
            second = low[layer, group] + code / 15.0 * span[layer, group]
            second = 0.95 * second + 0.05 * turn * turn
            moment_new[layer, :, lanes] = mean
            second_new[layer, :, lanes] = second
            scaled = (mean / (jnp.sqrt(second) + 1e-08)).astype(BF16)
            for copy in range(4):
                out[copy, layer, group * 16 : group * 16 + 16] = scaled
            lows.append(jnp.min(second, axis=0, keepdims=True))
            highs.append(jnp.max(second, axis=0, keepdims=True))
        lows = jnp.min(jnp.concatenate(lows, axis=0), axis=1, keepdims=True)
        highs = jnp.max(jnp.concatenate(highs, axis=0), axis=1, keepdims=True)
        tile = ends_tile(jnp.concatenate([lows, highs], axis=0))
        for copy in range(4):
            for to in range(2):
                out[copy, to, 128 + layer * 16 : 144 + layer * 16] = tile


def moments(got, moment, codes, low, span):
    return pl.pallas_call(
        moments_kernel,
        out_shape=(
            shape(4, 2, 160, 128),
            shape(2, 16, 1024, of=F32),
            shape(2, 16, 1024, of=F32),
        ),
        in_specs=[ANY, VMEM, VMEM, SMEM, SMEM],
        out_specs=(VMEM, VMEM, VMEM),
        scratch_shapes=[pltpu.VMEM((4, 2, 16, 1024), BF16), pltpu.SemaphoreType.DMA((1,))],
        compiler_params=PARAMS,
    )(got, moment, codes, low, span)


def back_kernel(got, right, out, held, sems):
    wait = pull([got], [held], sems)
    wait()
    rows = [held[:, at * 16 : at * 16 + 16, :].reshape(128, 128) for at in range(8)]
    returned = lax.dot_general(
        jnp.concatenate(rows, axis=1), right[...], (((1,), (1,)), ((), ())), preferred_element_type=F32
    ).astype(BF16)
    tiles = [
        ends_tile(jnp.concatenate(ends_of(held[:, at : at + 16, :]), axis=0)) for at in (128, 144)
    ]
    for copy in range(8):
        out[copy, 0:128] = returned[:, 0:128]
        out[copy, 128:256] = returned[:, 128:256]
        out[copy, 256:272] = tiles[0]
        out[copy, 272:288] = tiles[1]


def back_part(got, right):
    return pl.pallas_call(
        back_kernel,
        out_shape=shape(8, 288, 128),
        in_specs=[ANY, VMEM],
        out_specs=VMEM,
        scratch_shapes=[pltpu.VMEM((8, 160, 128), BF16), pltpu.SemaphoreType.DMA((1,))],
        compiler_params=PARAMS,
    )(got, right)


def update_kernel(got, left, out, ends, held, sems):
    wait = pull([got], [held], sems)
    wait()
    halves = [
        jnp.dot(left[...], held[:, at : at + 128, :].reshape(1024, 128), preferred_element_type=F32)
        for at in (0, 128)
    ]
    moved = jnp.concatenate(halves, axis=1).astype(BF16).reshape(8, 16, 256)
    for copy in range(8):
        out[copy] = moved
    for layer in range(2):
        low, high = ends_of(held[:, 256 + 16 * layer : 272 + 16 * layer, :])
        ends[0, layer] = jnp.broadcast_to(low, (8, 128))
        ends[1, layer] = jnp.broadcast_to(high, (8, 128))


def update_part(got, left):
    return pl.pallas_call(
        update_kernel,
        out_shape=(shape(8, 8, 16, 256), shape(2, 2, 8, 128, of=F32)),
        in_specs=[ANY, VMEM],
        out_specs=(VMEM, VMEM),
        scratch_shapes=[pltpu.VMEM((8, 288, 128), BF16), pltpu.SemaphoreType.DMA((1,))],
        compiler_params=PARAMS,
    )(got, left)


def step_kernel(got, olds, params_new, update, held, sems):
    rep = lax.axis_index("rep")
    lane = lax.broadcasted_iota(jnp.int32, (32, 128), 1)
    wait = pull([got], [held], sems)
    wait()

    def change_of(block, half):
        lanes = slice(half * 128, half * 128 + 128)
        tiles = [held[block, x, :, :, lanes].astype(F32).reshape(32, 128) for x in range(4)]
        return [tile.reshape(2, 16, 128) for tile in quarters(tiles, lane)]

    for half in range(2):
        for part, change in enumerate(change_of(rep, half)):
            start = half * 512 + part * 128
            update[:, :, start : start + 128] = change
        for block in range(8):
            for part, change in enumerate(change_of(block, half)):
                start = half * 512 + part * 128
                old = olds[jnp.bitwise_xor(rep, block), :, :, start : start + 128].astype(F32)
                new = old * (1.0 - 0.05 * 0.1) - 0.05 * change
                start += block * 1024
                params_new[:, :, start : start + 128] = new.astype(BF16)


def step(got, olds):
    return pl.pallas_call(
        step_kernel,
        out_shape=(shape(2, 16, 8192), shape(2, 16, 1024, of=F32)),
        in_specs=[ANY, VMEM],
        out_specs=(VMEM, VMEM),
        scratch_shapes=[pltpu.VMEM((8, 4, 2, 16, 256), BF16), pltpu.SemaphoreType.DMA((1,))],
        compiler_params=PARAMS,
    )(got, olds)


def on_device(grads, params, left_basis, right_basis, moment, codes, level_low, level_span):
    core = lax.axis_index("core")
    pick = lambda values, at: lax.dynamic_index_in_dim(values, at, 0, keepdims=False)
    both = lambda here, there: jnp.where(core == 0, jnp.stack([here, there]), jnp.stack([there, here]))
    swap = lambda values: shift(values, "core", 2, 1)
    tie = lax.optimization_barrier

    right = both(pick(right_basis, core), swap(pick(right_basis, 1 - core))).reshape(32, 1024)
    far = shift(right, "y", 8, 4)
    pair = jnp.stack([right, far])
    up, down = shift(pair, "y", 8, 1), shift(pair, "y", 8, -1)

    sent = panels(grads[0], left_basis)
    got = exchange(sent.reshape(64, 16, 384), ZQ)
    got, up, down = tie((got, up, down))
    part, left_y = left_part(got.reshape(8, 128, 384))
    more = shift(up, "y", 8, 1)

    flip = lambda values, axis, size, bit: lax.ppermute(values, axis, [(i, i ^ bit) for i in range(size)])

    def joined(olds, other, bit):
        return jnp.stack([olds, other], 1).reshape(8 // bit, 2, 16, 1024)

    olds = params[None]

    got = exchange(part.reshape(8, 128, 256), "y")
    turned, right_x = right_part(got, (right, far, up, down, more))
    turned, other = tie((turned, flip(tie((olds, part))[0], "rep", 8, 4)))
    olds = joined(olds, other, 4)
    got = exchange(turned.reshape(8, 16, 1024), Q).reshape(4, 2, 16, 1024)
    block, moment_new, second_new = moments(got, moment, codes, level_low, level_span)
    got = exchange(block.reshape(8, 160, 128), Q)
    block = back_part(got, right_x)
    got = exchange(block, "y")
    moved, ends = update_part(got, left_y)
    moved, other = tie((moved, flip(tie((olds, block))[0], "rep", 8, 2)))
    olds = joined(olds, other, 2)
    olds = joined(olds, flip(olds, "rep", 8, 1), 1)
    got = exchange(moved.reshape(64, 16, 256), ZQ).reshape(8, 4, 2, 16, 256)

    low_new = ends[0, :, :, 0]
    span_new = ends[1, :, :, 0] - low_new
    grouped = second_new.reshape(2, 16, 8, 128)
    levels = 15.0 * (grouped - low_new[:, None, :, None]) / span_new[:, None, :, None]
    levels = levels.reshape(2, 16, 1024)
    params_new, update = step(got, olds)
    return (params_new, moment_new, update, levels, low_new, span_new)


def solution(mesh):
    fine = Mesh(mesh.devices.reshape(8, 8, 4, 2), ("rep", "y", "x", "core"))
    return jax.shard_map(
        on_device,
        mesh=fine,
        in_specs=(
            P("rep", None, F, None),
            P(None, F, "rep"),
            P(None, F, None),
            P(None, ("rep",) + F, None),
            P(None, F, "rep"),
            P(None, F, "rep"),
            P(None, "rep"),
            P(None, "rep"),
        ),
        out_specs=(
            P(None, F, None),
            P(None, F, "rep"),
            P(None, F, "rep"),
            P(None, F, "rep"),
            P(None, "rep"),
            P(None, "rep"),
        ),
        check_vma=False,
    )
```

```python
import jax
import jax.numpy as jnp
from jax import lax
from jax.experimental import pallas as pl
from jax.experimental.pallas import tpu as pltpu
from jax.sharding import Mesh, PartitionSpec as P

F = ("pair", "odd", "x", "core")
A = ("odd", "x")
ZB = ("rep", "pair", "core")
B = ("pair", "core")
BF16, F32 = jnp.bfloat16, jnp.float32
VMEM = pl.BlockSpec(memory_space=pltpu.VMEM)
ANY = pl.BlockSpec(memory_space=pl.ANY)
PARAMS = pltpu.CompilerParams(vmem_limit_bytes=32 * 1024 * 1024)


def shape(*dims, of=BF16):
    return jax.ShapeDtypeStruct(dims, of)


def exchange(blocks, axes):
    return lax.all_to_all(blocks, axes, split_axis=0, concat_axis=0, tiled=True)


def shift(block, axis, size, by):
    return lax.ppermute(block, axis, [(i, (i + by) % size) for i in range(size)])


def pull(refs, places, sems):
    copies = [
        pltpu.make_async_copy(ref, place, sems.at[i])
        for i, (ref, place) in enumerate(zip(refs, places))
    ]
    for copy in copies:
        copy.start()

    def wait():
        for copy in copies:
            copy.wait()

    return wait


def panels_kernel(grads, left, out):
    eighth = pl.ds(pl.multiple_of(lax.axis_index("rep") * 128, 128), 128)
    basis = left[:, :, eighth]
    for panel in range(32):
        out[panel, :, :, 0:256] = grads[:, :, panel * 256 : panel * 256 + 256]
        out[panel, :, :, 256:384] = basis


def panels(grads, left):
    return pl.pallas_call(
        panels_kernel, out_shape=shape(32, 2, 16, 384), in_specs=[VMEM, VMEM], out_specs=VMEM
    )(grads, left)


def left_kernel(grads, out, left, held, sems):
    wait = pull([grads], [held], sems)
    wait()
    total = held[0, :, 0:256].astype(F32)
    for replica in range(1, 8):
        total += held[replica, :, 0:256].astype(F32)
    for replica in range(8):
        left[:, replica * 128 : replica * 128 + 128] = held[replica, :, 256:384]
    part = lax.dot_general(
        left[...], total.astype(BF16), (((0,), (0,)), ((), ())), preferred_element_type=F32
    )
    part = part.astype(BF16)
    for to in range(8):
        for pair in range(4):
            start = pair * 256 + to * 32
            out[to, pair * 32 : pair * 32 + 32] = part[start : start + 32]


def left_part(grads):
    return pl.pallas_call(
        left_kernel,
        out_shape=(shape(8, 128, 256), shape(128, 1024)),
        in_specs=[ANY],
        out_specs=(VMEM, VMEM),
        scratch_shapes=[pltpu.VMEM((8, 128, 384), BF16), pltpu.SemaphoreType.DMA((1,))],
        compiler_params=PARAMS,
    )(grads)


def right_kernel(got, near, away, out, right_out, held, right, sems):
    odd, x = lax.axis_index("odd"), lax.axis_index("x")
    ring, places = [], []
    for bits in range(8):
        block = (near, away)[bits % 2]
        ring.append(block.at[bits // 4, bits // 2 % 2])
        to = jnp.bitwise_xor(odd, bits // 4) * 4 + jnp.bitwise_xor(x, bits % 4)
        places.append(right.at[to])
    wait = pull([got] + ring, [held] + places, sems)
    wait()
    total = held[0].astype(F32)
    for part in range(1, 8):
        total += held[part].astype(F32)
    basis = right[...].reshape(256, 1024)
    out[...] = jnp.dot(total.astype(BF16), basis, preferred_element_type=F32).astype(BF16)
    right_out[...] = basis


def right_part(got, near, away):
    return pl.pallas_call(
        right_kernel,
        out_shape=(shape(128, 1024), shape(256, 1024)),
        in_specs=[ANY] * 3,
        out_specs=(VMEM, VMEM),
        scratch_shapes=[
            pltpu.VMEM((8, 128, 256), BF16),
            pltpu.VMEM((8, 32, 1024), BF16),
            pltpu.SemaphoreType.DMA((9,)),
        ],
        compiler_params=PARAMS,
    )(got, near, away)


def ends_tile(layers):
    lane = lax.broadcasted_iota(jnp.int32, (16, 128), 1)
    tile = jnp.zeros((16, 128), F32)
    for layer, ends in enumerate(layers):
        first = ends.astype(BF16).astype(F32)
        second = (ends - first).astype(BF16).astype(F32)
        third = ends - first - second
        for i, piece in enumerate((first, second, third)):
            tile = jnp.where(lane == layer * 3 + i, piece, tile)
    return tile.astype(BF16)


def ends_of(tiles):
    values = tiles.astype(F32)
    lane = lax.broadcasted_iota(jnp.int32, values.shape, 2)
    layers = []
    for mine in (lane < 3, lane >= 3):
        total = jnp.sum(jnp.where(mine, values, 0.0), axis=2, keepdims=True)
        layers.append((jnp.min(total[:, 0:8], axis=0), jnp.max(total[:, 8:16], axis=0)))
    return layers


def moments_kernel(got, moment, codes, low, span, out, moment_new, second_new, held, sems):
    wait = pull([got], [held], sems)
    wait()
    ends = []
    for layer in range(2):
        lows, highs = [], []
        for group in range(8):
            lanes = slice(group * 128, group * 128 + 128)
            turn = held[0, layer, :, lanes].astype(F32)
            for part in range(1, 4):
                turn += held[part, layer, :, lanes].astype(F32)
            mean = 0.9 * moment[layer, :, lanes] + 0.1 * turn
            code = codes[layer, :, lanes].astype(F32)
            at = (slice(layer, layer + 1), slice(group, group + 1))
            second = low[at] + code / 15.0 * span[at]
            second = 0.95 * second + 0.05 * turn * turn
            moment_new[layer, :, lanes] = mean
            second_new[layer, :, lanes] = second
            scaled = (mean / (jnp.sqrt(second) + 1e-08)).astype(BF16)
            for copy in range(4):
                out[copy, layer, group * 16 : group * 16 + 16] = scaled
            lows.append(jnp.min(second, axis=0, keepdims=True))
            highs.append(jnp.max(second, axis=0, keepdims=True))
        lows = jnp.min(jnp.concatenate(lows, axis=0), axis=1, keepdims=True)
        highs = jnp.max(jnp.concatenate(highs, axis=0), axis=1, keepdims=True)
        ends.append(jnp.concatenate([lows, highs], axis=0))
    tile = ends_tile(ends)
    for copy in range(4):
        for to in range(2):
            out[copy, to, 128:144] = tile


def moments(got, moment, codes, low, span):
    return pl.pallas_call(
        moments_kernel,
        out_shape=(
            shape(4, 2, 144, 128),
            shape(2, 16, 1024, of=F32),
            shape(2, 16, 1024, of=F32),
        ),
        in_specs=[ANY] + [VMEM] * 4,
        out_specs=(VMEM, VMEM, VMEM),
        scratch_shapes=[pltpu.VMEM((4, 2, 16, 1024), BF16), pltpu.SemaphoreType.DMA((1,))],
        compiler_params=PARAMS,
    )(got, moment, codes, low, span)


def back_kernel(got, right, out, held, sems):
    wait = pull([got], [held], sems)
    wait()
    rows = [held[:, at * 16 : at * 16 + 16, :].reshape(128, 128) for at in range(8)]
    returned = lax.dot_general(
        jnp.concatenate(rows, axis=1), right[...], (((1,), (1,)), ((), ())), preferred_element_type=F32
    ).astype(BF16)
    tile = ends_tile([jnp.concatenate(ends, axis=0) for ends in ends_of(held[:, 128:144, :])])
    for copy in range(8):
        out[copy, 0:128] = returned[:, 0:128]
        out[copy, 128:256] = returned[:, 128:256]
        out[copy, 256:272] = tile


def back_part(got, right):
    return pl.pallas_call(
        back_kernel,
        out_shape=shape(8, 272, 128),
        in_specs=[ANY, VMEM],
        out_specs=VMEM,
        scratch_shapes=[pltpu.VMEM((8, 144, 128), BF16), pltpu.SemaphoreType.DMA((1,))],
        compiler_params=PARAMS,
    )(got, right)


def update_kernel(got, left, out, ends, held, back, sems):
    wait = pull([got], [held], sems)
    wait()
    for half in range(2):
        for pair in range(4):
            start = half * 128 + pair * 32
            rows = held[:, start : start + 32, :].reshape(256, 128)
            back[pair * 256 : pair * 256 + 256, half * 128 : half * 128 + 128] = rows
    moved = jnp.dot(left[...], back[...], preferred_element_type=F32).astype(BF16).reshape(8, 16, 256)
    for copy in range(8):
        out[copy] = moved
    for layer, (low, high) in enumerate(ends_of(held[:, 256:272, :])):
        ends[0, layer] = jnp.broadcast_to(low, (8, 128))
        ends[1, layer] = jnp.broadcast_to(high, (8, 128))


def update_part(got, left):
    return pl.pallas_call(
        update_kernel,
        out_shape=(shape(8, 8, 16, 256), shape(2, 2, 8, 128, of=F32)),
        in_specs=[ANY, VMEM],
        out_specs=(VMEM, VMEM),
        scratch_shapes=[
            pltpu.VMEM((8, 272, 128), BF16),
            pltpu.VMEM((1024, 256), BF16),
            pltpu.SemaphoreType.DMA((1,)),
        ],
        compiler_params=PARAMS,
    )(got, left)


def step_kernel(got, olds, params_new, update, held, sems):
    rep = lax.axis_index("rep")
    wait = pull([got], [held], sems)
    wait()
    for panel in range(4):
        lanes = slice(panel * 256, panel * 256 + 256)
        update[:, :, lanes] = held[rep, panel].astype(F32)
        for block in range(8):
            change = held[block, panel].astype(F32)
            old = olds[jnp.bitwise_xor(rep, block), :, :, lanes].astype(F32)
            new = old * (1.0 - 0.05 * 0.1) - 0.05 * change
            start = block * 1024 + panel * 256
            params_new[:, :, start : start + 256] = new.astype(BF16)


def step(got, olds):
    return pl.pallas_call(
        step_kernel,
        out_shape=(shape(2, 16, 8192), shape(2, 16, 1024, of=F32)),
        in_specs=[ANY, VMEM],
        out_specs=(VMEM, VMEM),
        scratch_shapes=[pltpu.VMEM((8, 4, 2, 16, 256), BF16), pltpu.SemaphoreType.DMA((1,))],
        compiler_params=PARAMS,
    )(got, olds)


def on_device(grads, params, left_basis, right_basis, moment, codes, level_low, level_span):
    core = lax.axis_index("core")
    pick = lambda values, at: lax.dynamic_index_in_dim(values, at, 0, keepdims=False)
    both = lambda here, there: jnp.where(core == 0, jnp.stack([here, there]), jnp.stack([there, here]))
    swap = lambda values: shift(values, "core", 2, 1)
    flip = lambda values, axis, size, bit: lax.ppermute(values, axis, [(i, i ^ bit) for i in range(size)])
    tie = lax.optimization_barrier

    right = both(pick(right_basis, core), swap(pick(right_basis, 1 - core))).reshape(1, 32, 1024)
    right = jnp.concatenate([right, flip(right, "x", 4, 2)])[None]
    near = jnp.concatenate([right, flip(right, "odd", 2, 1)])
    away = flip(near, "x", 4, 1)

    sent = panels(grads[0], left_basis)
    got = exchange(sent.reshape(64, 16, 384), ZB)
    got, near = tie((got, near))
    part, left_rows = left_part(got.reshape(8, 128, 384))

    def joined(olds, other, bit):
        return jnp.stack([olds, other], 1).reshape(8 // bit, 2, 16, 1024)

    olds = params[None]

    got = exchange(part, A)
    turned, right_rows = right_part(got, near, away)
    turned, other = tie((turned, flip(tie((olds, part))[0], "rep", 8, 4)))
    olds = joined(olds, other, 4)
    got = exchange(turned.reshape(8, 16, 1024), B).reshape(4, 2, 16, 1024)
    block, moment_new, second_new = moments(got, moment, codes, level_low, level_span)
    got = exchange(block.reshape(8, 144, 128), B)
    block = back_part(got, right_rows)
    got = exchange(block, A)
    moved, ends = update_part(got, left_rows)
    moved, other = tie((moved, flip(tie((olds, block))[0], "rep", 8, 2)))
    olds = joined(olds, other, 2)
    olds = joined(olds, flip(olds, "rep", 8, 1), 1)
    got = exchange(moved.reshape(64, 16, 256), ZB).reshape(8, 4, 2, 16, 256)

    low_new = ends[0, :, :, 0]
    span_new = ends[1, :, :, 0] - low_new
    grouped = second_new.reshape(2, 16, 8, 128)
    levels = 15.0 * (grouped - low_new[:, None, :, None]) / span_new[:, None, :, None]
    levels = levels.reshape(2, 16, 1024)
    params_new, update = step(got, olds)
    return (params_new, moment_new, update, levels, low_new, span_new)


def solution(mesh):
    fine = Mesh(mesh.devices.reshape(8, 4, 2, 4, 2), ("rep",) + F)
    return jax.shard_map(
        on_device,
        mesh=fine,
        in_specs=(
            P("rep", None, F, None),
            P(None, F, "rep"),
            P(None, F, None),
            P(None, ("rep",) + F, None),
            P(None, F, "rep"),
            P(None, F, "rep"),
            P(None, "rep"),
            P(None, "rep"),
        ),
        out_specs=(
            P(None, F, None),
            P(None, F, "rep"),
            P(None, F, "rep"),
            P(None, F, "rep"),
            P(None, "rep"),
            P(None, "rep"),
        ),
        check_vma=False,
    )
```

```python
import jax
import jax.numpy as jnp
from jax import lax
from jax.experimental import pallas as pl
from jax.experimental.pallas import tpu as pltpu
from jax.sharding import Mesh, PartitionSpec as P

F = ("pair", "odd", "x", "core")
A = ("x", "core")
ZB = ("rep", "pair", "odd")
B = ("pair", "odd")
BF16, F32 = jnp.bfloat16, jnp.float32
VMEM = pl.BlockSpec(memory_space=pltpu.VMEM)
ANY = pl.BlockSpec(memory_space=pl.ANY)
PARAMS = pltpu.CompilerParams(vmem_limit_bytes=32 * 1024 * 1024)


def shape(*dims, of=BF16):
    return jax.ShapeDtypeStruct(dims, of)


def exchange(blocks, axes):
    return lax.all_to_all(blocks, axes, split_axis=0, concat_axis=0, tiled=True)


def shift(block, axis, size, by):
    return lax.ppermute(block, axis, [(i, (i + by) % size) for i in range(size)])


def pull(refs, places, sems):
    copies = [
        pltpu.make_async_copy(ref, place, sems.at[i])
        for i, (ref, place) in enumerate(zip(refs, places))
    ]
    for copy in copies:
        copy.start()

    def wait():
        for copy in copies:
            copy.wait()

    return wait


def panels_kernel(grads, left, out):
    eighth = pl.ds(pl.multiple_of(lax.axis_index("rep") * 128, 128), 128)
    basis = left[:, :, eighth]
    for panel in range(32):
        out[panel, :, :, 0:256] = grads[:, :, panel * 256 : panel * 256 + 256]
        out[panel, :, :, 256:384] = basis


def panels(grads, left):
    return pl.pallas_call(
        panels_kernel, out_shape=shape(32, 2, 16, 384), in_specs=[VMEM, VMEM], out_specs=VMEM
    )(grads, left)


def left_kernel(grads, out, left, held, sems):
    wait = pull([grads], [held], sems)
    wait()
    total = held[0, :, 0:256].astype(F32)
    for replica in range(1, 8):
        total += held[replica, :, 0:256].astype(F32)
    for replica in range(8):
        left[:, replica * 128 : replica * 128 + 128] = held[replica, :, 256:384]
    part = lax.dot_general(
        left[...], total.astype(BF16), (((0,), (0,)), ((), ())), preferred_element_type=F32
    )
    part = part.astype(BF16)
    for to in range(8):
        for y in range(8):
            start = y * 128 + to * 16
            out[to, y * 16 : y * 16 + 16] = part[start : start + 16]


def left_part(grads):
    return pl.pallas_call(
        left_kernel,
        out_shape=(shape(8, 128, 256), shape(128, 1024)),
        in_specs=[ANY],
        out_specs=(VMEM, VMEM),
        scratch_shapes=[pltpu.VMEM((8, 128, 384), BF16), pltpu.SemaphoreType.DMA((1,))],
        compiler_params=PARAMS,
    )(grads)


def right_kernel(got, near, away, other, out, right_out, held, right, sems):
    at, odd = lax.axis_index("x") * 2 + lax.axis_index("core"), lax.axis_index("odd")
    ring, places = [], []
    for bits in range(8):
        block = (near, away)[bits // 2 % 2]
        to = jnp.bitwise_xor(at, bits)
        ring.append(block.at[bits // 4, bits % 2, odd])
        places.append(right.at[odd, to])
        ring.append(other.at[bits // 2 % 2, bits // 4, bits % 2])
        places.append(right.at[1 - odd, to])
    wait = pull([got] + ring, [held] + places, sems)
    wait()
    total = held[0].astype(F32)
    for part in range(1, 8):
        total += held[part].astype(F32)
    basis = right[...].reshape(256, 1024)
    out[...] = jnp.dot(total.astype(BF16), basis, preferred_element_type=F32).astype(BF16)
    right_out[...] = basis


def right_part(got, near, away, other):
    return pl.pallas_call(
        right_kernel,
        out_shape=(shape(128, 1024), shape(256, 1024)),
        in_specs=[ANY] * 4,
        out_specs=(VMEM, VMEM),
        scratch_shapes=[
            pltpu.VMEM((8, 128, 256), BF16),
            pltpu.VMEM((2, 8, 16, 1024), BF16),
            pltpu.SemaphoreType.DMA((17,)),
        ],
        compiler_params=PARAMS,
    )(got, near, away, other)


def ends_tile(layers):
    lane = lax.broadcasted_iota(jnp.int32, (16, 128), 1)
    tile = jnp.zeros((16, 128), F32)
    for layer, ends in enumerate(layers):
        first = ends.astype(BF16).astype(F32)
        second = (ends - first).astype(BF16).astype(F32)
        third = ends - first - second
        for i, piece in enumerate((first, second, third)):
            tile = jnp.where(lane == layer * 3 + i, piece, tile)
    return tile.astype(BF16)


def ends_of(tiles):
    values = tiles.astype(F32)
    lane = lax.broadcasted_iota(jnp.int32, values.shape, 2)
    layers = []
    for mine in (lane < 3, lane >= 3):
        total = jnp.sum(jnp.where(mine, values, 0.0), axis=2, keepdims=True)
        layers.append((jnp.min(total[:, 0:8], axis=0), jnp.max(total[:, 8:16], axis=0)))
    return layers


def moments_kernel(got, moment, codes, low, span, out, moment_new, second_new, held, sems):
    wait = pull([got], [held], sems)
    wait()
    ends = []
    for layer in range(2):
        lows, highs = [], []
        for group in range(8):
            lanes = slice(group * 128, group * 128 + 128)
            turn = held[0, layer, :, lanes].astype(F32)
            for part in range(1, 4):
                turn += held[part, layer, :, lanes].astype(F32)
            mean = 0.9 * moment[layer, :, lanes] + 0.1 * turn
            code = codes[layer, :, lanes].astype(F32)
            at = (slice(layer, layer + 1), slice(group, group + 1))
            second = low[at] + code / 15.0 * span[at]
            second = 0.95 * second + 0.05 * turn * turn
            moment_new[layer, :, lanes] = mean
            second_new[layer, :, lanes] = second
            scaled = (mean / (jnp.sqrt(second) + 1e-08)).astype(BF16)
            for copy in range(4):
                out[copy, layer, group * 16 : group * 16 + 16] = scaled
            lows.append(jnp.min(second, axis=0, keepdims=True))
            highs.append(jnp.max(second, axis=0, keepdims=True))
        lows = jnp.min(jnp.concatenate(lows, axis=0), axis=1, keepdims=True)
        highs = jnp.max(jnp.concatenate(highs, axis=0), axis=1, keepdims=True)
        ends.append(jnp.concatenate([lows, highs], axis=0))
    tile = ends_tile(ends)
    for copy in range(4):
        for to in range(2):
            out[copy, to, 128:144] = tile


def moments(got, moment, codes, low, span):
    return pl.pallas_call(
        moments_kernel,
        out_shape=(
            shape(4, 2, 144, 128),
            shape(2, 16, 1024, of=F32),
            shape(2, 16, 1024, of=F32),
        ),
        in_specs=[ANY] + [VMEM] * 4,
        out_specs=(VMEM, VMEM, VMEM),
        scratch_shapes=[pltpu.VMEM((4, 2, 16, 1024), BF16), pltpu.SemaphoreType.DMA((1,))],
        compiler_params=PARAMS,
    )(got, moment, codes, low, span)


def back_kernel(got, right, out, held, sems):
    wait = pull([got], [held], sems)
    wait()
    rows = [held[:, at * 16 : at * 16 + 16, :].reshape(128, 128) for at in range(8)]
    returned = lax.dot_general(
        jnp.concatenate(rows, axis=1), right[...], (((1,), (1,)), ((), ())), preferred_element_type=F32
    ).astype(BF16)
    tile = ends_tile([jnp.concatenate(ends, axis=0) for ends in ends_of(held[:, 128:144, :])])
    for copy in range(8):
        out[copy, 0:128] = returned[:, 0:128]
        out[copy, 128:256] = returned[:, 128:256]
        out[copy, 256:272] = tile


def back_part(got, right):
    return pl.pallas_call(
        back_kernel,
        out_shape=shape(8, 272, 128),
        in_specs=[ANY, VMEM],
        out_specs=VMEM,
        scratch_shapes=[pltpu.VMEM((8, 144, 128), BF16), pltpu.SemaphoreType.DMA((1,))],
        compiler_params=PARAMS,
    )(got, right)


def update_kernel(got, left, out, ends, held, back, sems):
    wait = pull([got], [held], sems)
    wait()
    for half in range(2):
        for y in range(8):
            start = half * 128 + y * 16
            rows = held[:, start : start + 16, :].reshape(128, 128)
            back[y * 128 : y * 128 + 128, half * 128 : half * 128 + 128] = rows
    moved = jnp.dot(left[...], back[...], preferred_element_type=F32).astype(BF16).reshape(8, 16, 256)
    for copy in range(8):
        out[copy] = moved
    for layer, (low, high) in enumerate(ends_of(held[:, 256:272, :])):
        ends[0, layer] = jnp.broadcast_to(low, (8, 128))
        ends[1, layer] = jnp.broadcast_to(high, (8, 128))


def update_part(got, left):
    return pl.pallas_call(
        update_kernel,
        out_shape=(shape(8, 8, 16, 256), shape(2, 2, 8, 128, of=F32)),
        in_specs=[ANY, VMEM],
        out_specs=(VMEM, VMEM),
        scratch_shapes=[
            pltpu.VMEM((8, 272, 128), BF16),
            pltpu.VMEM((1024, 256), BF16),
            pltpu.SemaphoreType.DMA((1,)),
        ],
        compiler_params=PARAMS,
    )(got, left)


def step_kernel(got, olds, params_new, update, held, sems):
    rep = lax.axis_index("rep")
    wait = pull([got], [held], sems)
    wait()
    for panel in range(4):
        lanes = slice(panel * 256, panel * 256 + 256)
        update[:, :, lanes] = held[rep, panel].astype(F32)
        for block in range(8):
            change = held[block, panel].astype(F32)
            old = olds[jnp.bitwise_xor(rep, block), :, :, lanes].astype(F32)
            new = old * (1.0 - 0.05 * 0.1) - 0.05 * change
            start = block * 1024 + panel * 256
            params_new[:, :, start : start + 256] = new.astype(BF16)


def step(got, olds):
    return pl.pallas_call(
        step_kernel,
        out_shape=(shape(2, 16, 8192), shape(2, 16, 1024, of=F32)),
        in_specs=[ANY, VMEM],
        out_specs=(VMEM, VMEM),
        scratch_shapes=[pltpu.VMEM((8, 4, 2, 16, 256), BF16), pltpu.SemaphoreType.DMA((1,))],
        compiler_params=PARAMS,
    )(got, olds)


def on_device(grads, params, left_basis, right_basis, moment, codes, level_low, level_span):
    odd = lax.axis_index("odd")
    flip = lambda values, axis, size, bit: lax.ppermute(values, axis, [(i, i ^ bit) for i in range(size)])
    tie = lax.optimization_barrier

    near = jnp.stack([right_basis, flip(right_basis, "core", 2, 1)])
    near = jnp.stack([near, flip(near, "x", 4, 2)])
    away = flip(near, "x", 4, 1)

    sent = panels(grads[0], left_basis)
    got = exchange(sent.reshape(64, 16, 384), ZB)
    got, away = tie((got, away))
    part, left_rows = left_part(got.reshape(8, 128, 384))

    def joined(olds, other, bit):
        return jnp.stack([olds, other], 1).reshape(8 // bit, 2, 16, 1024)

    olds = params[None]

    layer = lambda values: lax.dynamic_index_in_dim(values, 1 - odd, 2, keepdims=False)
    other = flip(jnp.stack([layer(near), layer(away)]), "odd", 2, 1)

    got = exchange(part, A)
    turned, right_rows = right_part(got, near, away, other)
    turned, other = tie((turned, flip(tie((olds, part))[0], "rep", 8, 4)))
    olds = joined(olds, other, 4)
    got = exchange(turned.reshape(8, 16, 1024), B).reshape(4, 2, 16, 1024)
    block, moment_new, second_new = moments(got, moment, codes, level_low, level_span)
    got = exchange(block.reshape(8, 144, 128), B)
    block = back_part(got, right_rows)
    got = exchange(block, A)
    moved, ends = update_part(got, left_rows)
    moved, other = tie((moved, flip(tie((olds, block))[0], "rep", 8, 2)))
    olds = joined(olds, other, 2)
    olds = joined(olds, flip(olds, "rep", 8, 1), 1)
    got = exchange(moved.reshape(64, 16, 256), ZB).reshape(8, 4, 2, 16, 256)

    low_new = ends[0, :, :, 0]
    span_new = ends[1, :, :, 0] - low_new
    grouped = second_new.reshape(2, 16, 8, 128)
    levels = 15.0 * (grouped - low_new[:, None, :, None]) / span_new[:, None, :, None]
    levels = levels.reshape(2, 16, 1024)
    params_new, update = step(got, olds)
    return (params_new, moment_new, update, levels, low_new, span_new)


def solution(mesh):
    fine = Mesh(mesh.devices.reshape(8, 4, 2, 4, 2), ("rep",) + F)
    return jax.shard_map(
        on_device,
        mesh=fine,
        in_specs=(
            P("rep", None, F, None),
            P(None, F, "rep"),
            P(None, F, None),
            P(None, ("rep",) + F, None),
            P(None, F, "rep"),
            P(None, F, "rep"),
            P(None, "rep"),
            P(None, "rep"),
        ),
        out_specs=(
            P(None, F, None),
            P(None, F, "rep"),
            P(None, F, "rep"),
            P(None, F, "rep"),
            P(None, "rep"),
            P(None, "rep"),
        ),
        check_vma=False,
    )
```

```python
import jax
import jax.numpy as jnp
from jax import lax
from jax.experimental import pallas as pl
from jax.experimental.pallas import tpu as pltpu
from jax.sharding import Mesh, PartitionSpec as P

F = ("pair", "odd", "x", "core")
A = ("x", "core")
ZB = ("rep", "pair", "odd")
B = ("pair", "odd")
BF16, F32 = jnp.bfloat16, jnp.float32
VMEM = pl.BlockSpec(memory_space=pltpu.VMEM)
ANY = pl.BlockSpec(memory_space=pl.ANY)
PARAMS = pltpu.CompilerParams(vmem_limit_bytes=32 * 1024 * 1024)


def shape(*dims, of=BF16):
    return jax.ShapeDtypeStruct(dims, of)


def exchange(blocks, axes):
    return lax.all_to_all(blocks, axes, split_axis=0, concat_axis=0, tiled=True)


def shift(block, axis, size, by):
    return lax.ppermute(block, axis, [(i, (i + by) % size) for i in range(size)])


def pull(refs, places, sems):
    copies = [
        pltpu.make_async_copy(ref, place, sems.at[i])
        for i, (ref, place) in enumerate(zip(refs, places))
    ]
    for copy in copies:
        copy.start()

    def wait():
        for copy in copies:
            copy.wait()

    return wait


def panels_kernel(grads, left, out):
    eighth = pl.ds(pl.multiple_of(lax.axis_index("rep") * 128, 128), 128)
    basis = left[:, :, eighth]
    for panel in range(32):
        out[panel, :, :, 0:256] = grads[:, :, panel * 256 : panel * 256 + 256]
        out[panel, :, :, 256:384] = basis


def panels(grads, left):
    return pl.pallas_call(
        panels_kernel, out_shape=shape(32, 2, 16, 384), in_specs=[VMEM, VMEM], out_specs=VMEM
    )(grads, left)


def left_kernel(grads, low, span, out, left, levels, held, sems):
    wait = pull([grads], [held], sems)
    for which, values in enumerate((low, span)):
        for layer in range(2):
            for group in range(8):
                value = values[layer : layer + 1, group : group + 1]
                levels[which, layer, group : group + 1, :] = jnp.broadcast_to(value, (1, 128))
    wait()
    total = held[0, :, 0:256].astype(F32)
    for replica in range(1, 8):
        total += held[replica, :, 0:256].astype(F32)
    for replica in range(8):
        left[:, replica * 128 : replica * 128 + 128] = held[replica, :, 256:384]
    part = lax.dot_general(
        left[...], total.astype(BF16), (((0,), (0,)), ((), ())), preferred_element_type=F32
    )
    part = part.astype(BF16)
    for to in range(8):
        for y in range(8):
            start = y * 128 + to * 16
            out[to, y * 16 : y * 16 + 16] = part[start : start + 16]


def left_part(grads, low, span):
    return pl.pallas_call(
        left_kernel,
        out_shape=(shape(8, 128, 256), shape(128, 1024), shape(2, 2, 8, 128, of=F32)),
        in_specs=[ANY, VMEM, VMEM],
        out_specs=(VMEM,) * 3,
        scratch_shapes=[pltpu.VMEM((8, 128, 384), BF16), pltpu.SemaphoreType.DMA((1,))],
        compiler_params=PARAMS,
    )(grads, low, span)


def right_kernel(got, near, away, other, out, right_out, held, right, sems):
    at, odd = lax.axis_index("x") * 2 + lax.axis_index("core"), lax.axis_index("odd")
    ring, places = [], []
    for bits in range(8):
        block = (near, away)[bits // 2 % 2]
        to = jnp.bitwise_xor(at, bits)
        ring.append(block.at[bits // 4, bits % 2, odd])
        places.append(right.at[odd, to])
        ring.append(other.at[bits // 2 % 2, bits // 4, bits % 2])
        places.append(right.at[1 - odd, to])
    wait = pull([got] + ring, [held] + places, sems)
    wait()
    total = held[0].astype(F32)
    for part in range(1, 8):
        total += held[part].astype(F32)
    basis = right[...].reshape(256, 1024)
    out[...] = jnp.dot(total.astype(BF16), basis, preferred_element_type=F32).astype(BF16)
    right_out[...] = basis


def right_part(got, near, away, other):
    return pl.pallas_call(
        right_kernel,
        out_shape=(shape(128, 1024), shape(256, 1024)),
        in_specs=[ANY] * 4,
        out_specs=(VMEM, VMEM),
        scratch_shapes=[
            pltpu.VMEM((8, 128, 256), BF16),
            pltpu.VMEM((2, 8, 16, 1024), BF16),
            pltpu.SemaphoreType.DMA((17,)),
        ],
        compiler_params=PARAMS,
    )(got, near, away, other)


def ends_tile(layers):
    lane = lax.broadcasted_iota(jnp.int32, (16, 128), 1)
    tile = jnp.zeros((16, 128), F32)
    for layer, ends in enumerate(layers):
        first = ends.astype(BF16).astype(F32)
        second = (ends - first).astype(BF16).astype(F32)
        third = ends - first - second
        for i, piece in enumerate((first, second, third)):
            tile = jnp.where(lane == layer * 3 + i, piece, tile)
    return tile.astype(BF16)


def ends_of(tiles):
    values = tiles.astype(F32)
    lane = lax.broadcasted_iota(jnp.int32, values.shape, 2)
    layers = []
    for mine in (lane < 3, lane >= 3):
        total = jnp.sum(jnp.where(mine, values, 0.0), axis=2, keepdims=True)
        layers.append((jnp.min(total[:, 0:8], axis=0), jnp.max(total[:, 8:16], axis=0)))
    return layers


def moments_kernel(got, moment, codes, levels, params, out, moment_new, second_new, held, sems):
    wait = pull([got], [held], sems)
    wait()
    ends = []
    for layer in range(2):
        lows, highs = [], []
        for group in range(8):
            lanes = slice(group * 128, group * 128 + 128)
            turn = held[0, layer, :, lanes].astype(F32)
            for part in range(1, 4):
                turn += held[part, layer, :, lanes].astype(F32)
            mean = 0.9 * moment[layer, :, lanes] + 0.1 * turn
            code = codes[layer, :, lanes].astype(F32)
            low = levels[0, layer, group : group + 1]
            second = low + code / 15.0 * levels[1, layer, group : group + 1]
            second = 0.95 * second + 0.05 * turn * turn
            moment_new[layer, :, lanes] = mean
            second_new[layer, :, lanes] = second
            scaled = (mean / (jnp.sqrt(second) + 1e-08)).astype(BF16)
            for copy in range(4):
                out[copy, layer, group * 16 : group * 16 + 16] = scaled
            lows.append(jnp.min(second, axis=0, keepdims=True))
            highs.append(jnp.max(second, axis=0, keepdims=True))
        lows = jnp.min(jnp.concatenate(lows, axis=0), axis=1, keepdims=True)
        highs = jnp.max(jnp.concatenate(highs, axis=0), axis=1, keepdims=True)
        ends.append(jnp.concatenate([lows, highs], axis=0))
    tile = ends_tile(ends)
    for copy in range(4):
        for to in range(2):
            out[copy, to, 128:144] = tile
            for half in range(2):
                start = copy * 256 + half * 128
                out[copy, to, 144 + half * 16 : 160 + half * 16] = params[to, :, start : start + 128]


def moments(got, moment, codes, levels, params):
    return pl.pallas_call(
        moments_kernel,
        out_shape=(
            shape(4, 2, 176, 128),
            shape(2, 16, 1024, of=F32),
            shape(2, 16, 1024, of=F32),
        ),
        in_specs=[ANY] + [VMEM] * 4,
        out_specs=(VMEM, VMEM, VMEM),
        scratch_shapes=[pltpu.VMEM((4, 2, 16, 1024), BF16), pltpu.SemaphoreType.DMA((1,))],
        compiler_params=PARAMS,
    )(got, moment, codes, levels, params)


def back_kernel(got, right, out, params, held, sems):
    wait = pull([got], [held], sems)
    wait()
    rows = [held[:, at * 16 : at * 16 + 16, :].reshape(128, 128) for at in range(8)]
    returned = lax.dot_general(
        jnp.concatenate(rows, axis=1), right[...], (((1,), (1,)), ((), ())), preferred_element_type=F32
    ).astype(BF16)
    for half in range(2):
        rows = held[:, 144 + half * 16 : 160 + half * 16, :].reshape(128, 128)
        params[:, half * 128 : half * 128 + 128] = rows
    tile = ends_tile([jnp.concatenate(ends, axis=0) for ends in ends_of(held[:, 128:144, :])])
    for copy in range(8):
        out[copy, 0:128] = returned[:, 0:128]
        out[copy, 128:256] = returned[:, 128:256]
        out[copy, 256:272] = tile


def back_part(got, right):
    return pl.pallas_call(
        back_kernel,
        out_shape=(shape(8, 272, 128), shape(128, 256)),
        in_specs=[ANY, VMEM],
        out_specs=(VMEM, VMEM),
        scratch_shapes=[pltpu.VMEM((8, 176, 128), BF16), pltpu.SemaphoreType.DMA((1,))],
        compiler_params=PARAMS,
    )(got, right)


def update_kernel(got, left, params, out, ends, held, back, sems):
    wait = pull([got], [held], sems)
    wait()
    for half in range(2):
        for y in range(8):
            start = half * 128 + y * 16
            rows = held[:, start : start + 16, :].reshape(128, 128)
            back[y * 128 : y * 128 + 128, half * 128 : half * 128 + 128] = rows
    moved = jnp.dot(left[...], back[...], preferred_element_type=F32)
    new = params[...].astype(F32) * (1.0 - 0.05 * 0.1) - 0.05 * moved
    new = new.astype(BF16).reshape(8, 16, 256)
    for copy in range(8):
        out[copy] = new
    out[lax.axis_index("rep")] = moved.astype(BF16).reshape(8, 16, 256)
    for layer, (low, high) in enumerate(ends_of(held[:, 256:272, :])):
        ends[0, layer] = jnp.broadcast_to(low, (8, 128))
        ends[1, layer] = jnp.broadcast_to(high, (8, 128))


def update_part(got, left, params):
    return pl.pallas_call(
        update_kernel,
        out_shape=(shape(8, 8, 16, 256), shape(2, 2, 8, 128, of=F32)),
        in_specs=[ANY, VMEM, VMEM],
        out_specs=(VMEM, VMEM),
        scratch_shapes=[
            pltpu.VMEM((8, 272, 128), BF16),
            pltpu.VMEM((1024, 256), BF16),
            pltpu.SemaphoreType.DMA((1,)),
        ],
        compiler_params=PARAMS,
    )(got, left, params)


def step_kernel(got, params, second, ends, params_new, update, levels, low_new, span_new, held, sems):
    rep = lax.axis_index("rep")
    wait = pull([got], [held], sems)
    wait()
    for panel in range(4):
        for block in range(8):
            start = block * 1024 + panel * 256
            params_new[:, :, start : start + 256] = held[block, panel]
    for panel in range(4):
        lanes = slice(panel * 256, panel * 256 + 256)
        change = held[rep, panel].astype(F32)
        update[:, :, lanes] = change
        new = params[:, :, lanes].astype(F32) * (1.0 - 0.05 * 0.1) - 0.05 * change
        own = pl.ds(pl.multiple_of(rep * 1024 + panel * 256, 256), 256)
        params_new[:, :, own] = new.astype(BF16)
    row = lax.broadcasted_iota(jnp.int32, (8, 128), 0)
    lane = lax.broadcasted_iota(jnp.int32, (8, 128), 1)
    for layer in range(2):
        low = ends[0, layer]
        span = ends[1, layer] - low
        for out, values in ((low_new, low), (span_new, span)):
            spread = jnp.sum(jnp.where(row == lane, values, 0.0), axis=0, keepdims=True)
            out[layer : layer + 1, :] = spread[:, 0:8]
        for group in range(8):
            lanes = slice(group * 128, group * 128 + 128)
            above = second[layer, :, lanes] - low[group : group + 1]
            levels[layer, :, lanes] = 15.0 * above / span[group : group + 1]


def step(got, params, second, ends):
    return pl.pallas_call(
        step_kernel,
        out_shape=(
            shape(2, 16, 8192),
            shape(2, 16, 1024, of=F32),
            shape(2, 16, 1024, of=F32),
            shape(2, 8, of=F32),
            shape(2, 8, of=F32),
        ),
        in_specs=[ANY, VMEM, VMEM, VMEM],
        out_specs=(VMEM,) * 5,
        scratch_shapes=[pltpu.VMEM((8, 4, 2, 16, 256), BF16), pltpu.SemaphoreType.DMA((1,))],
        compiler_params=PARAMS,
    )(got, params, second, ends)


def on_device(grads, params, left_basis, right_basis, moment, codes, level_low, level_span):
    odd = lax.axis_index("odd")
    flip = lambda values, axis, size, bit: lax.ppermute(values, axis, [(i, i ^ bit) for i in range(size)])
    tie = lax.optimization_barrier

    near = jnp.stack([right_basis, flip(right_basis, "core", 2, 1)])
    near = jnp.stack([near, flip(near, "x", 4, 2)])
    away = flip(near, "x", 4, 1)

    sent = panels(grads[0], left_basis)
    got = exchange(sent.reshape(64, 16, 384), ZB)
    got, away = tie((got, away))
    part, left_rows, spread = left_part(got.reshape(8, 128, 384), level_low, level_span)

    layer = lambda values: lax.dynamic_index_in_dim(values, 1 - odd, 2, keepdims=False)
    other = flip(jnp.stack([layer(near), layer(away)]), "odd", 2, 1)

    got = exchange(part, A)
    turned, right_rows = right_part(got, near, away, other)
    got = exchange(turned.reshape(8, 16, 1024), B).reshape(4, 2, 16, 1024)
    block, moment_new, second_new = moments(got, moment, codes, spread, params)
    got = exchange(block.reshape(8, 176, 128), B)
    block, old = back_part(got, right_rows)
    got = exchange(block, A)
    moved, ends = update_part(got, left_rows, old)
    got = exchange(moved.reshape(64, 16, 256), ZB).reshape(8, 4, 2, 16, 256)

    params_new, update, levels, low_new, span_new = step(got, params, second_new, ends)
    return (params_new, moment_new, update, levels, low_new, span_new)


def solution(mesh):
    fine = Mesh(mesh.devices.reshape(8, 4, 2, 4, 2), ("rep",) + F)
    return jax.shard_map(
        on_device,
        mesh=fine,
        in_specs=(
            P("rep", None, F, None),
            P(None, F, "rep"),
            P(None, F, None),
            P(None, ("rep",) + F, None),
            P(None, F, "rep"),
            P(None, F, "rep"),
            P(None, "rep"),
            P(None, "rep"),
        ),
        out_specs=(
            P(None, F, None),
            P(None, F, "rep"),
            P(None, F, "rep"),
            P(None, F, "rep"),
            P(None, "rep"),
            P(None, "rep"),
        ),
        check_vma=False,
    )
```

```python
import jax
import jax.numpy as jnp
from jax import lax
from jax.experimental import pallas as pl
from jax.experimental.pallas import tpu as pltpu
from jax.sharding import Mesh, PartitionSpec as P

F = ("pair", "odd", "x", "core")
A = ("x", "core")
ZB = ("rep", "pair", "odd")
B = ("pair", "odd")
BF16, F32 = jnp.bfloat16, jnp.float32
VMEM = pl.BlockSpec(memory_space=pltpu.VMEM)
ANY = pl.BlockSpec(memory_space=pl.ANY)
PARAMS = pltpu.CompilerParams(vmem_limit_bytes=32 * 1024 * 1024)


def shape(*dims, of=BF16):
    return jax.ShapeDtypeStruct(dims, of)


def exchange(blocks, axes):
    return lax.all_to_all(blocks, axes, split_axis=0, concat_axis=0, tiled=True)


def shift(block, axis, size, by):
    return lax.ppermute(block, axis, [(i, (i + by) % size) for i in range(size)])


def pull(refs, places, sems):
    copies = [
        pltpu.make_async_copy(ref, place, sems.at[i])
        for i, (ref, place) in enumerate(zip(refs, places))
    ]
    for copy in copies:
        copy.start()

    def wait():
        for copy in copies:
            copy.wait()

    return wait


def panels_kernel(grads, left, out):
    eighth = pl.ds(pl.multiple_of(lax.axis_index("rep") * 128, 128), 128)
    basis = left[:, :, eighth]
    for panel in range(32):
        out[panel, :, :, 0:256] = grads[:, :, panel * 256 : panel * 256 + 256]
        out[panel, :, :, 256:384] = basis


def panels(grads, left):
    return pl.pallas_call(
        panels_kernel, out_shape=shape(32, 2, 16, 384), in_specs=[VMEM, VMEM], out_specs=VMEM
    )(grads, left)


def left_kernel(grads, low, span, out, left, levels, held, sems):
    wait = pull([grads], [held], sems)
    for which, values in enumerate((low, span)):
        for layer in range(2):
            for group in range(8):
                value = values[layer : layer + 1, group : group + 1]
                levels[which, layer, group : group + 1, :] = jnp.broadcast_to(value, (1, 128))
    wait()
    total = held[0, :, 0:256].astype(F32)
    for replica in range(1, 8):
        total += held[replica, :, 0:256].astype(F32)
    for replica in range(8):
        left[:, replica * 128 : replica * 128 + 128] = held[replica, :, 256:384]
    part = lax.dot_general(
        left[...], total.astype(BF16), (((0,), (0,)), ((), ())), preferred_element_type=F32
    )
    part = part.astype(BF16)
    for to in range(8):
        for y in range(8):
            start = y * 128 + to * 16
            out[to, y * 16 : y * 16 + 16] = part[start : start + 16]


def left_part(grads, low, span):
    return pl.pallas_call(
        left_kernel,
        out_shape=(shape(8, 128, 256), shape(128, 1024), shape(2, 2, 8, 128, of=F32)),
        in_specs=[ANY, VMEM, VMEM],
        out_specs=(VMEM,) * 3,
        scratch_shapes=[pltpu.VMEM((8, 128, 384), BF16), pltpu.SemaphoreType.DMA((1,))],
        compiler_params=PARAMS,
    )(grads, low, span)


def right_kernel(got, own, one, two, three, other, out, right_out, held, right, sems):
    at, odd = lax.axis_index("x") * 2 + lax.axis_index("core"), lax.axis_index("odd")
    ring, places = [], []
    for bits in range(8):
        block = (own, one, two, three)[bits // 2]
        to = jnp.bitwise_xor(at, bits)
        ring.append(block.at[bits % 2, odd])
        places.append(right.at[odd, to])
        ring.append(other.at[bits // 2, bits % 2])
        places.append(right.at[1 - odd, to])
    wait = pull([got] + ring, [held] + places, sems)
    wait()
    total = held[0].astype(F32)
    for part in range(1, 8):
        total += held[part].astype(F32)
    basis = right[...].reshape(256, 1024)
    out[...] = jnp.dot(total.astype(BF16), basis, preferred_element_type=F32).astype(BF16)
    right_out[...] = basis


def right_part(got, rights, other):
    return pl.pallas_call(
        right_kernel,
        out_shape=(shape(128, 1024), shape(256, 1024)),
        in_specs=[ANY] * 6,
        out_specs=(VMEM, VMEM),
        scratch_shapes=[
            pltpu.VMEM((8, 128, 256), BF16),
            pltpu.VMEM((2, 8, 16, 1024), BF16),
            pltpu.SemaphoreType.DMA((17,)),
        ],
        compiler_params=PARAMS,
    )(got, *rights, other)


def ends_tile(layers):
    lane = lax.broadcasted_iota(jnp.int32, (16, 128), 1)
    tile = jnp.zeros((16, 128), F32)
    for layer, ends in enumerate(layers):
        first = ends.astype(BF16).astype(F32)
        second = (ends - first).astype(BF16).astype(F32)
        third = ends - first - second
        for i, piece in enumerate((first, second, third)):
            tile = jnp.where(lane == layer * 3 + i, piece, tile)
    return tile.astype(BF16)


def ends_of(tiles):
    values = tiles.astype(F32)
    lane = lax.broadcasted_iota(jnp.int32, values.shape, 2)
    layers = []
    for mine in (lane < 3, lane >= 3):
        total = jnp.sum(jnp.where(mine, values, 0.0), axis=2, keepdims=True)
        layers.append((jnp.min(total[:, 0:8], axis=0), jnp.max(total[:, 8:16], axis=0)))
    return layers


def moments_kernel(got, moment, codes, levels, params, out, moment_new, second_new, held, sems):
    wait = pull([got], [held], sems)
    wait()
    ends = []
    for layer in range(2):
        lows, highs = [], []
        for group in range(8):
            lanes = slice(group * 128, group * 128 + 128)
            turn = held[0, layer, :, lanes].astype(F32)
            for part in range(1, 4):
                turn += held[part, layer, :, lanes].astype(F32)
            mean = 0.9 * moment[layer, :, lanes] + 0.1 * turn
            code = codes[layer, :, lanes].astype(F32)
            low = levels[0, layer, group : group + 1]
            second = low + code / 15.0 * levels[1, layer, group : group + 1]
            second = 0.95 * second + 0.05 * turn * turn
            moment_new[layer, :, lanes] = mean
            second_new[layer, :, lanes] = second
            scaled = (mean / (jnp.sqrt(second) + 1e-08)).astype(BF16)
            for copy in range(4):
                out[copy, layer, group * 16 : group * 16 + 16] = scaled
            lows.append(jnp.min(second, axis=0, keepdims=True))
            highs.append(jnp.max(second, axis=0, keepdims=True))
        lows = jnp.min(jnp.concatenate(lows, axis=0), axis=1, keepdims=True)
        highs = jnp.max(jnp.concatenate(highs, axis=0), axis=1, keepdims=True)
        ends.append(jnp.concatenate([lows, highs], axis=0))
    tile = ends_tile(ends)
    for copy in range(4):
        for to in range(2):
            out[copy, to, 128:144] = tile
            for half in range(2):
                start = copy * 256 + half * 128
                out[copy, to, 144 + half * 16 : 160 + half * 16] = params[to, :, start : start + 128]


def moments(got, moment, codes, levels, params):
    return pl.pallas_call(
        moments_kernel,
        out_shape=(
            shape(4, 2, 176, 128),
            shape(2, 16, 1024, of=F32),
            shape(2, 16, 1024, of=F32),
        ),
        in_specs=[ANY] + [VMEM] * 4,
        out_specs=(VMEM, VMEM, VMEM),
        scratch_shapes=[pltpu.VMEM((4, 2, 16, 1024), BF16), pltpu.SemaphoreType.DMA((1,))],
        compiler_params=PARAMS,
    )(got, moment, codes, levels, params)


def back_kernel(got, right, out, params, held, sems):
    wait = pull([got], [held], sems)
    wait()
    rows = [held[:, at * 16 : at * 16 + 16, :].reshape(128, 128) for at in range(8)]
    returned = lax.dot_general(
        jnp.concatenate(rows, axis=1), right[...], (((1,), (1,)), ((), ())), preferred_element_type=F32
    ).astype(BF16)
    for half in range(2):
        rows = held[:, 144 + half * 16 : 160 + half * 16, :].reshape(128, 128)
        params[:, half * 128 : half * 128 + 128] = rows
    tile = ends_tile([jnp.concatenate(ends, axis=0) for ends in ends_of(held[:, 128:144, :])])
    for copy in range(8):
        out[copy, 0:128] = returned[:, 0:128]
        out[copy, 128:256] = returned[:, 128:256]
        out[copy, 256:272] = tile


def back_part(got, right):
    return pl.pallas_call(
        back_kernel,
        out_shape=(shape(8, 272, 128), shape(128, 256)),
        in_specs=[ANY, VMEM],
        out_specs=(VMEM, VMEM),
        scratch_shapes=[pltpu.VMEM((8, 176, 128), BF16), pltpu.SemaphoreType.DMA((1,))],
        compiler_params=PARAMS,
    )(got, right)


def update_kernel(got, left, params, out, ends, held, back, sems):
    wait = pull([got], [held], sems)
    wait()
    for half in range(2):
        for y in range(8):
            start = half * 128 + y * 16
            rows = held[:, start : start + 16, :].reshape(128, 128)
            back[y * 128 : y * 128 + 128, half * 128 : half * 128 + 128] = rows
    moved = jnp.dot(left[...], back[...], preferred_element_type=F32)
    new = params[...].astype(F32) * (1.0 - 0.05 * 0.1) - 0.05 * moved
    new = new.astype(BF16).reshape(8, 16, 256)
    for copy in range(8):
        out[copy] = new
    out[lax.axis_index("rep")] = moved.astype(BF16).reshape(8, 16, 256)
    for layer, (low, high) in enumerate(ends_of(held[:, 256:272, :])):
        ends[0, layer] = jnp.broadcast_to(low, (8, 128))
        ends[1, layer] = jnp.broadcast_to(high, (8, 128))


def update_part(got, left, params):
    return pl.pallas_call(
        update_kernel,
        out_shape=(shape(8, 8, 16, 256), shape(2, 2, 8, 128, of=F32)),
        in_specs=[ANY, VMEM, VMEM],
        out_specs=(VMEM, VMEM),
        scratch_shapes=[
            pltpu.VMEM((8, 272, 128), BF16),
            pltpu.VMEM((1024, 256), BF16),
            pltpu.SemaphoreType.DMA((1,)),
        ],
        compiler_params=PARAMS,
    )(got, left, params)


def step_kernel(got, params, second, ends, params_new, update, levels, low_new, span_new, held, sems):
    rep = lax.axis_index("rep")
    wait = pull([got], [held], sems)
    wait()
    for panel in range(4):
        for block in range(8):
            start = block * 1024 + panel * 256
            params_new[:, :, start : start + 256] = held[block, panel]
    for panel in range(4):
        lanes = slice(panel * 256, panel * 256 + 256)
        change = held[rep, panel].astype(F32)
        update[:, :, lanes] = change
        new = params[:, :, lanes].astype(F32) * (1.0 - 0.05 * 0.1) - 0.05 * change
        own = pl.ds(pl.multiple_of(rep * 1024 + panel * 256, 256), 256)
        params_new[:, :, own] = new.astype(BF16)
    row = lax.broadcasted_iota(jnp.int32, (8, 128), 0)
    lane = lax.broadcasted_iota(jnp.int32, (8, 128), 1)
    for layer in range(2):
        low = ends[0, layer]
        span = ends[1, layer] - low
        for out, values in ((low_new, low), (span_new, span)):
            spread = jnp.sum(jnp.where(row == lane, values, 0.0), axis=0, keepdims=True)
            out[layer : layer + 1, :] = spread[:, 0:8]
        for group in range(8):
            lanes = slice(group * 128, group * 128 + 128)
            above = second[layer, :, lanes] - low[group : group + 1]
            levels[layer, :, lanes] = 15.0 * above / span[group : group + 1]


def step(got, params, second, ends):
    return pl.pallas_call(
        step_kernel,
        out_shape=(
            shape(2, 16, 8192),
            shape(2, 16, 1024, of=F32),
            shape(2, 16, 1024, of=F32),
            shape(2, 8, of=F32),
            shape(2, 8, of=F32),
        ),
        in_specs=[ANY, VMEM, VMEM, VMEM],
        out_specs=(VMEM,) * 5,
        scratch_shapes=[pltpu.VMEM((8, 4, 2, 16, 256), BF16), pltpu.SemaphoreType.DMA((1,))],
        compiler_params=PARAMS,
    )(got, params, second, ends)


def on_device(grads, params, left_basis, right_basis, moment, codes, level_low, level_span):
    odd = lax.axis_index("odd")
    flip = lambda values, axis, size, bit: lax.ppermute(values, axis, [(i, i ^ bit) for i in range(size)])
    tie = lax.optimization_barrier

    near = jnp.stack([right_basis, flip(right_basis, "core", 2, 1)])
    rights = [near] + [flip(near, "x", 4, bits) for bits in (1, 2, 3)]

    sent = panels(grads[0], left_basis)
    got = exchange(sent.reshape(64, 16, 384), ZB)
    got, rights = tie((got, rights))
    part, left_rows, spread = left_part(got.reshape(8, 128, 384), level_low, level_span)

    layer = lambda values: lax.dynamic_index_in_dim(values, 1 - odd, 1, keepdims=False)
    other = flip(jnp.stack([layer(values) for values in rights]), "odd", 2, 1)

    got = exchange(part, A)
    turned, right_rows = right_part(got, rights, other)
    got = exchange(turned.reshape(8, 16, 1024), B).reshape(4, 2, 16, 1024)
    block, moment_new, second_new = moments(got, moment, codes, spread, params)
    got = exchange(block.reshape(8, 176, 128), B)
    block, old = back_part(got, right_rows)
    got = exchange(block, A)
    moved, ends = update_part(got, left_rows, old)
    got = exchange(moved.reshape(64, 16, 256), ZB).reshape(8, 4, 2, 16, 256)

    params_new, update, levels, low_new, span_new = step(got, params, second_new, ends)
    return (params_new, moment_new, update, levels, low_new, span_new)


def solution(mesh):
    fine = Mesh(mesh.devices.reshape(8, 4, 2, 4, 2), ("rep",) + F)
    return jax.shard_map(
        on_device,
        mesh=fine,
        in_specs=(
            P("rep", None, F, None),
            P(None, F, "rep"),
            P(None, F, None),
            P(None, ("rep",) + F, None),
            P(None, F, "rep"),
            P(None, F, "rep"),
            P(None, "rep"),
            P(None, "rep"),
        ),
        out_specs=(
            P(None, F, None),
            P(None, F, "rep"),
            P(None, F, "rep"),
            P(None, F, "rep"),
            P(None, "rep"),
            P(None, "rep"),
        ),
        check_vma=False,
    )
```

```python
import jax
import jax.numpy as jnp
from jax import lax
from jax.experimental import pallas as pl
from jax.experimental.pallas import tpu as pltpu
from jax.sharding import Mesh, PartitionSpec as P

F = ("pair", "odd", "x", "core")
A = ("x", "core")
ZB = ("rep", "pair", "odd")
B = ("pair", "odd")
BF16, F32 = jnp.bfloat16, jnp.float32
VMEM = pl.BlockSpec(memory_space=pltpu.VMEM)
ANY = pl.BlockSpec(memory_space=pl.ANY)
PARAMS = pltpu.CompilerParams(vmem_limit_bytes=32 * 1024 * 1024)


def shape(*dims, of=BF16):
    return jax.ShapeDtypeStruct(dims, of)


def exchange(blocks, axes):
    return lax.all_to_all(blocks, axes, split_axis=0, concat_axis=0, tiled=True)


def shift(block, axis, size, by):
    return lax.ppermute(block, axis, [(i, (i + by) % size) for i in range(size)])


def pull(refs, places, sems):
    copies = [
        pltpu.make_async_copy(ref, place, sems.at[i])
        for i, (ref, place) in enumerate(zip(refs, places))
    ]
    for copy in copies:
        copy.start()

    def wait():
        for copy in copies:
            copy.wait()

    return wait


def panels_kernel(grads, left, out):
    eighth = pl.ds(pl.multiple_of(lax.axis_index("rep") * 128, 128), 128)
    basis = left[:, :, eighth]
    for panel in range(32):
        out[panel, :, :, 0:256] = grads[:, :, panel * 256 : panel * 256 + 256]
        out[panel, :, :, 256:384] = basis


def panels(grads, left):
    return pl.pallas_call(
        panels_kernel, out_shape=shape(32, 2, 16, 384), in_specs=[VMEM, VMEM], out_specs=VMEM
    )(grads, left)


def left_kernel(grads, low, span, out, left, levels, held, sems):
    wait = pull([grads], [held], sems)
    for which, values in enumerate((low, span)):
        for layer in range(2):
            for group in range(8):
                value = values[layer : layer + 1, group : group + 1]
                levels[which, layer, group : group + 1, :] = jnp.broadcast_to(value, (1, 128))
    wait()
    total = held[0, :, 0:256].astype(F32)
    for replica in range(1, 8):
        total += held[replica, :, 0:256].astype(F32)
    for replica in range(8):
        left[:, replica * 128 : replica * 128 + 128] = held[replica, :, 256:384]
    part = lax.dot_general(
        left[...], total.astype(BF16), (((0,), (0,)), ((), ())), preferred_element_type=F32
    )
    part = part.astype(BF16)
    for to in range(8):
        for y in range(8):
            start = y * 128 + to * 16
            out[to, y * 16 : y * 16 + 16] = part[start : start + 16]


def left_part(grads, low, span):
    return pl.pallas_call(
        left_kernel,
        out_shape=(shape(8, 128, 256), shape(128, 1024), shape(2, 2, 8, 128, of=F32)),
        in_specs=[ANY, VMEM, VMEM],
        out_specs=(VMEM,) * 3,
        scratch_shapes=[pltpu.VMEM((8, 128, 384), BF16), pltpu.SemaphoreType.DMA((1,))],
        compiler_params=PARAMS,
    )(grads, low, span)


def right_kernel(got, own, one, two, three, other, out, right_out, held, right, sems):
    x, odd = lax.axis_index("x"), lax.axis_index("odd")
    ring, places = [], []
    for bits, block in enumerate((own, one, two, three)):
        to = jnp.bitwise_xor(x, bits)
        ring += [block.at[:, odd], other.at[bits]]
        places += [right.at[odd, to], right.at[1 - odd, to]]
    wait = pull([got] + ring, [held] + places, sems)
    wait()
    total = held[0].astype(F32)
    for part in range(1, 8):
        total += held[part].astype(F32)
    basis = right[...].reshape(256, 1024)
    out[...] = jnp.dot(total.astype(BF16), basis, preferred_element_type=F32).astype(BF16)
    right_out[...] = basis


def right_part(got, rights, other):
    return pl.pallas_call(
        right_kernel,
        out_shape=(shape(128, 1024), shape(256, 1024)),
        in_specs=[ANY] * 6,
        out_specs=(VMEM, VMEM),
        scratch_shapes=[
            pltpu.VMEM((8, 128, 256), BF16),
            pltpu.VMEM((2, 4, 2, 16, 1024), BF16),
            pltpu.SemaphoreType.DMA((9,)),
        ],
        compiler_params=PARAMS,
    )(got, *rights, other)


def ends_tile(layers):
    lane = lax.broadcasted_iota(jnp.int32, (16, 128), 1)
    tile = jnp.zeros((16, 128), F32)
    for layer, ends in enumerate(layers):
        first = ends.astype(BF16).astype(F32)
        second = (ends - first).astype(BF16).astype(F32)
        third = ends - first - second
        for i, piece in enumerate((first, second, third)):
            tile = jnp.where(lane == layer * 3 + i, piece, tile)
    return tile.astype(BF16)


def ends_of(tiles):
    values = tiles.astype(F32)
    lane = lax.broadcasted_iota(jnp.int32, values.shape, 2)
    layers = []
    for mine in (lane < 3, lane >= 3):
        total = jnp.sum(jnp.where(mine, values, 0.0), axis=2, keepdims=True)
        layers.append((jnp.min(total[:, 0:8], axis=0), jnp.max(total[:, 8:16], axis=0)))
    return layers


def moments_kernel(got, moment, codes, levels, params, out, moment_new, second_new, held, sems):
    wait = pull([got], [held], sems)
    wait()
    ends = []
    for layer in range(2):
        lows, highs = [], []
        for group in range(8):
            lanes = slice(group * 128, group * 128 + 128)
            turn = held[0, layer, :, lanes].astype(F32)
            for part in range(1, 4):
                turn += held[part, layer, :, lanes].astype(F32)
            mean = 0.9 * moment[layer, :, lanes] + 0.1 * turn
            code = codes[layer, :, lanes].astype(F32)
            low = levels[0, layer, group : group + 1]
            second = low + code / 15.0 * levels[1, layer, group : group + 1]
            second = 0.95 * second + 0.05 * turn * turn
            moment_new[layer, :, lanes] = mean
            second_new[layer, :, lanes] = second
            scaled = (mean / (jnp.sqrt(second) + 1e-08)).astype(BF16)
            for copy in range(4):
                out[copy, layer, group * 16 : group * 16 + 16] = scaled
            lows.append(jnp.min(second, axis=0, keepdims=True))
            highs.append(jnp.max(second, axis=0, keepdims=True))
        lows = jnp.min(jnp.concatenate(lows, axis=0), axis=1, keepdims=True)
        highs = jnp.max(jnp.concatenate(highs, axis=0), axis=1, keepdims=True)
        ends.append(jnp.concatenate([lows, highs], axis=0))
    tile = ends_tile(ends)
    for copy in range(4):
        for to in range(2):
            out[copy, to, 128:144] = tile
            for half in range(2):
                start = copy * 256 + half * 128
                out[copy, to, 144 + half * 16 : 160 + half * 16] = params[to, :, start : start + 128]


def moments(got, moment, codes, levels, params):
    return pl.pallas_call(
        moments_kernel,
        out_shape=(
            shape(4, 2, 176, 128),
            shape(2, 16, 1024, of=F32),
            shape(2, 16, 1024, of=F32),
        ),
        in_specs=[ANY] + [VMEM] * 4,
        out_specs=(VMEM, VMEM, VMEM),
        scratch_shapes=[pltpu.VMEM((4, 2, 16, 1024), BF16), pltpu.SemaphoreType.DMA((1,))],
        compiler_params=PARAMS,
    )(got, moment, codes, levels, params)


def back_kernel(got, right, out, params, held, sems):
    wait = pull([got], [held], sems)
    wait()
    rows = [held[:, at * 16 : at * 16 + 16, :].reshape(128, 128) for at in range(8)]
    returned = lax.dot_general(
        jnp.concatenate(rows, axis=1), right[...], (((1,), (1,)), ((), ())), preferred_element_type=F32
    ).astype(BF16)
    for half in range(2):
        rows = held[:, 144 + half * 16 : 160 + half * 16, :].reshape(128, 128)
        params[:, half * 128 : half * 128 + 128] = rows
    tile = ends_tile([jnp.concatenate(ends, axis=0) for ends in ends_of(held[:, 128:144, :])])
    for copy in range(8):
        out[copy, 0:128] = returned[:, 0:128]
        out[copy, 128:256] = returned[:, 128:256]
        out[copy, 256:272] = tile


def back_part(got, right):
    return pl.pallas_call(
        back_kernel,
        out_shape=(shape(8, 272, 128), shape(128, 256)),
        in_specs=[ANY, VMEM],
        out_specs=(VMEM, VMEM),
        scratch_shapes=[pltpu.VMEM((8, 176, 128), BF16), pltpu.SemaphoreType.DMA((1,))],
        compiler_params=PARAMS,
    )(got, right)


def update_kernel(got, left, params, out, ends, held, back, sems):
    wait = pull([got], [held], sems)
    wait()
    for half in range(2):
        for y in range(8):
            start = half * 128 + y * 16
            rows = held[:, start : start + 16, :].reshape(128, 128)
            back[y * 128 : y * 128 + 128, half * 128 : half * 128 + 128] = rows
    moved = jnp.dot(left[...], back[...], preferred_element_type=F32)
    new = params[...].astype(F32) * (1.0 - 0.05 * 0.1) - 0.05 * moved
    new = new.astype(BF16).reshape(8, 16, 256)
    for copy in range(8):
        out[copy] = new
    out[lax.axis_index("rep")] = moved.astype(BF16).reshape(8, 16, 256)
    for layer, (low, high) in enumerate(ends_of(held[:, 256:272, :])):
        ends[0, layer] = jnp.broadcast_to(low, (8, 128))
        ends[1, layer] = jnp.broadcast_to(high, (8, 128))


def update_part(got, left, params):
    return pl.pallas_call(
        update_kernel,
        out_shape=(shape(8, 8, 16, 256), shape(2, 2, 8, 128, of=F32)),
        in_specs=[ANY, VMEM, VMEM],
        out_specs=(VMEM, VMEM),
        scratch_shapes=[
            pltpu.VMEM((8, 272, 128), BF16),
            pltpu.VMEM((1024, 256), BF16),
            pltpu.SemaphoreType.DMA((1,)),
        ],
        compiler_params=PARAMS,
    )(got, left, params)


def step_kernel(got, params, second, ends, params_new, update, levels, low_new, span_new, held, sems):
    rep = lax.axis_index("rep")
    wait = pull([got], [held], sems)
    wait()
    for panel in range(4):
        for block in range(8):
            start = block * 1024 + panel * 256
            params_new[:, :, start : start + 256] = held[block, panel]
    for panel in range(4):
        lanes = slice(panel * 256, panel * 256 + 256)
        change = held[rep, panel].astype(F32)
        update[:, :, lanes] = change
        new = params[:, :, lanes].astype(F32) * (1.0 - 0.05 * 0.1) - 0.05 * change
        own = pl.ds(pl.multiple_of(rep * 1024 + panel * 256, 256), 256)
        params_new[:, :, own] = new.astype(BF16)
    row = lax.broadcasted_iota(jnp.int32, (8, 128), 0)
    lane = lax.broadcasted_iota(jnp.int32, (8, 128), 1)
    for layer in range(2):
        low = ends[0, layer]
        span = ends[1, layer] - low
        for out, values in ((low_new, low), (span_new, span)):
            spread = jnp.sum(jnp.where(row == lane, values, 0.0), axis=0, keepdims=True)
            out[layer : layer + 1, :] = spread[:, 0:8]
        for group in range(8):
            lanes = slice(group * 128, group * 128 + 128)
            above = second[layer, :, lanes] - low[group : group + 1]
            levels[layer, :, lanes] = 15.0 * above / span[group : group + 1]


def step(got, params, second, ends):
    return pl.pallas_call(
        step_kernel,
        out_shape=(
            shape(2, 16, 8192),
            shape(2, 16, 1024, of=F32),
            shape(2, 16, 1024, of=F32),
            shape(2, 8, of=F32),
            shape(2, 8, of=F32),
        ),
        in_specs=[ANY, VMEM, VMEM, VMEM],
        out_specs=(VMEM,) * 5,
        scratch_shapes=[pltpu.VMEM((8, 4, 2, 16, 256), BF16), pltpu.SemaphoreType.DMA((1,))],
        compiler_params=PARAMS,
    )(got, params, second, ends)


def on_device(grads, params, left_basis, right_basis, moment, codes, level_low, level_span):
    odd = lax.axis_index("odd")
    flip = lambda values, axis, size, bit: lax.ppermute(values, axis, [(i, i ^ bit) for i in range(size)])
    tie = lax.optimization_barrier

    near = flip(right_basis, "core", 2, 1)
    near = jnp.where(
        lax.axis_index("core") == 0, jnp.stack([right_basis, near]), jnp.stack([near, right_basis])
    )
    rights = [near] + [flip(near, "x", 4, bits) for bits in (1, 2, 3)]

    sent = panels(grads[0], left_basis)
    got = exchange(sent.reshape(64, 16, 384), ZB)
    got, rights = tie((got, rights))
    part, left_rows, spread = left_part(got.reshape(8, 128, 384), level_low, level_span)

    layer = lambda values: lax.dynamic_index_in_dim(values, 1 - odd, 1, keepdims=False)
    other = flip(jnp.stack([layer(values) for values in rights]), "odd", 2, 1)

    got = exchange(part, A)
    turned, right_rows = right_part(got, rights, other)
    got = exchange(turned.reshape(8, 16, 1024), B).reshape(4, 2, 16, 1024)
    block, moment_new, second_new = moments(got, moment, codes, spread, params)
    got = exchange(block.reshape(8, 176, 128), B)
    block, old = back_part(got, right_rows)
    got = exchange(block, A)
    moved, ends = update_part(got, left_rows, old)
    got = exchange(moved.reshape(64, 16, 256), ZB).reshape(8, 4, 2, 16, 256)

    params_new, update, levels, low_new, span_new = step(got, params, second_new, ends)
    return (params_new, moment_new, update, levels, low_new, span_new)


def solution(mesh):
    fine = Mesh(mesh.devices.reshape(8, 4, 2, 4, 2), ("rep",) + F)
    return jax.shard_map(
        on_device,
        mesh=fine,
        in_specs=(
            P("rep", None, F, None),
            P(None, F, "rep"),
            P(None, F, None),
            P(None, ("rep",) + F, None),
            P(None, F, "rep"),
            P(None, F, "rep"),
            P(None, "rep"),
            P(None, "rep"),
        ),
        out_specs=(
            P(None, F, None),
            P(None, F, "rep"),
            P(None, F, "rep"),
            P(None, F, "rep"),
            P(None, "rep"),
            P(None, "rep"),
        ),
        check_vma=False,
    )
```

```python
import jax
import jax.numpy as jnp
from jax import lax
from jax.experimental import pallas as pl
from jax.experimental.pallas import tpu as pltpu
from jax.sharding import Mesh, PartitionSpec as P

F = ("pair", "odd", "x", "core")
A = ("x", "core")
ZB = ("rep", "pair", "odd")
B = ("pair", "odd")
BF16, F32 = jnp.bfloat16, jnp.float32
VMEM = pl.BlockSpec(memory_space=pltpu.VMEM)
ANY = pl.BlockSpec(memory_space=pl.ANY)
PARAMS = pltpu.CompilerParams(vmem_limit_bytes=32 * 1024 * 1024)


def shape(*dims, of=BF16):
    return jax.ShapeDtypeStruct(dims, of)


def exchange(blocks, axes):
    return lax.all_to_all(blocks, axes, split_axis=0, concat_axis=0, tiled=True)


def shift(block, axis, size, by):
    return lax.ppermute(block, axis, [(i, (i + by) % size) for i in range(size)])


def pull(refs, places, sems):
    copies = [
        pltpu.make_async_copy(ref, place, sems.at[i])
        for i, (ref, place) in enumerate(zip(refs, places))
    ]
    for copy in copies:
        copy.start()

    def wait():
        for copy in copies:
            copy.wait()

    return wait


def panels_kernel(grads, left, out):
    eighth = pl.ds(pl.multiple_of(lax.axis_index("rep") * 128, 128), 128)
    basis = left[:, :, eighth]
    for panel in range(32):
        out[panel, :, :, 0:256] = grads[:, :, panel * 256 : panel * 256 + 256]
        out[panel, :, :, 256:384] = basis


def panels(grads, left):
    return pl.pallas_call(
        panels_kernel, out_shape=shape(32, 2, 16, 384), in_specs=[VMEM, VMEM], out_specs=VMEM
    )(grads, left)


def left_kernel(grads, low, span, out, left, levels, held, sems):
    wait = pull([grads], [held], sems)
    for which, values in enumerate((low, span)):
        for layer in range(2):
            for group in range(8):
                value = values[layer : layer + 1, group : group + 1]
                levels[which, layer, group : group + 1, :] = jnp.broadcast_to(value, (1, 128))
    wait()
    total = held[0, :, 0:256].astype(F32)
    for replica in range(1, 8):
        total += held[replica, :, 0:256].astype(F32)
    for replica in range(8):
        left[:, replica * 128 : replica * 128 + 128] = held[replica, :, 256:384]
    part = lax.dot_general(
        left[...], total.astype(BF16), (((0,), (0,)), ((), ())), preferred_element_type=F32
    )
    part = part.astype(BF16)
    for to in range(8):
        for y in range(8):
            start = y * 128 + to * 16
            out[to, y * 16 : y * 16 + 16] = part[start : start + 16]


def left_part(grads, low, span):
    return pl.pallas_call(
        left_kernel,
        out_shape=(shape(8, 128, 256), shape(128, 1024), shape(2, 2, 8, 128, of=F32)),
        in_specs=[ANY, VMEM, VMEM],
        out_specs=(VMEM,) * 3,
        scratch_shapes=[pltpu.VMEM((8, 128, 384), BF16), pltpu.SemaphoreType.DMA((1,))],
        compiler_params=PARAMS,
    )(grads, low, span)


def right_kernel(got, own, one, two, three, other, out, right, held, sems):
    x, odd = lax.axis_index("x"), lax.axis_index("odd")
    ring, places = [], []
    for bits, block in enumerate((own, one, two, three)):
        to = jnp.bitwise_xor(x, bits)
        ring += [block.at[:, odd], other.at[bits]]
        places += [right.at[odd, to], right.at[1 - odd, to]]
    wait = pull([got] + ring, [held] + places, sems)
    wait()
    total = held[0].astype(F32)
    for part in range(1, 8):
        total += held[part].astype(F32)
    basis = right[...].reshape(256, 1024)
    out[...] = jnp.dot(total.astype(BF16), basis, preferred_element_type=F32).astype(BF16)


def right_part(got, rights, other):
    return pl.pallas_call(
        right_kernel,
        out_shape=(shape(128, 1024), shape(2, 4, 2, 16, 1024)),
        in_specs=[ANY] * 6,
        out_specs=(VMEM, VMEM),
        scratch_shapes=[
            pltpu.VMEM((8, 128, 256), BF16),
            pltpu.SemaphoreType.DMA((9,)),
        ],
        compiler_params=PARAMS,
    )(got, *rights, other)


def ends_tile(layers):
    lane = lax.broadcasted_iota(jnp.int32, (16, 128), 1)
    tile = jnp.zeros((16, 128), F32)
    for layer, ends in enumerate(layers):
        first = ends.astype(BF16).astype(F32)
        second = (ends - first).astype(BF16).astype(F32)
        third = ends - first - second
        for i, piece in enumerate((first, second, third)):
            tile = jnp.where(lane == layer * 3 + i, piece, tile)
    return tile.astype(BF16)


def ends_of(tiles):
    values = tiles.astype(F32)
    lane = lax.broadcasted_iota(jnp.int32, values.shape, 2)
    layers = []
    for mine in (lane < 3, lane >= 3):
        total = jnp.sum(jnp.where(mine, values, 0.0), axis=2, keepdims=True)
        layers.append((jnp.min(total[:, 0:8], axis=0), jnp.max(total[:, 8:16], axis=0)))
    return layers


def moments_kernel(got, moment, codes, levels, params, out, moment_new, second_new, held, sems):
    wait = pull([got], [held], sems)
    wait()
    ends = []
    for layer in range(2):
        lows, highs = [], []
        for group in range(8):
            lanes = slice(group * 128, group * 128 + 128)
            turn = held[0, layer, :, lanes].astype(F32)
            for part in range(1, 4):
                turn += held[part, layer, :, lanes].astype(F32)
            mean = 0.9 * moment[layer, :, lanes] + 0.1 * turn
            code = codes[layer, :, lanes].astype(F32)
            low = levels[0, layer, group : group + 1]
            second = low + code / 15.0 * levels[1, layer, group : group + 1]
            second = 0.95 * second + 0.05 * turn * turn
            moment_new[layer, :, lanes] = mean
            second_new[layer, :, lanes] = second
            scaled = (mean / (jnp.sqrt(second) + 1e-08)).astype(BF16)
            for copy in range(4):
                out[copy, layer, group * 16 : group * 16 + 16] = scaled
            lows.append(jnp.min(second, axis=0, keepdims=True))
            highs.append(jnp.max(second, axis=0, keepdims=True))
        lows = jnp.min(jnp.concatenate(lows, axis=0), axis=1, keepdims=True)
        highs = jnp.max(jnp.concatenate(highs, axis=0), axis=1, keepdims=True)
        ends.append(jnp.concatenate([lows, highs], axis=0))
    tile = ends_tile(ends)
    for copy in range(4):
        for to in range(2):
            out[copy, to, 128:144] = tile
            for half in range(2):
                start = copy * 256 + half * 128
                out[copy, to, 144 + half * 16 : 160 + half * 16] = params[to, :, start : start + 128]


def moments(got, moment, codes, levels, params):
    return pl.pallas_call(
        moments_kernel,
        out_shape=(
            shape(4, 2, 176, 128),
            shape(2, 16, 1024, of=F32),
            shape(2, 16, 1024, of=F32),
        ),
        in_specs=[ANY] + [VMEM] * 4,
        out_specs=(VMEM, VMEM, VMEM),
        scratch_shapes=[pltpu.VMEM((4, 2, 16, 1024), BF16), pltpu.SemaphoreType.DMA((1,))],
        compiler_params=PARAMS,
    )(got, moment, codes, levels, params)


def back_kernel(got, right, out, params, held, sems):
    wait = pull([got], [held], sems)
    wait()
    rows = [held[:, at * 16 : at * 16 + 16, :].reshape(128, 128) for at in range(8)]
    returned = lax.dot_general(
        jnp.concatenate(rows, axis=1), right[...], (((1,), (1,)), ((), ())), preferred_element_type=F32
    ).astype(BF16)
    for half in range(2):
        rows = held[:, 144 + half * 16 : 160 + half * 16, :].reshape(128, 128)
        params[:, half * 128 : half * 128 + 128] = rows
    tile = ends_tile([jnp.concatenate(ends, axis=0) for ends in ends_of(held[:, 128:144, :])])
    for copy in range(8):
        out[copy, 0:128] = returned[:, 0:128]
        out[copy, 128:256] = returned[:, 128:256]
        out[copy, 256:272] = tile


def back_part(got, right):
    return pl.pallas_call(
        back_kernel,
        out_shape=(shape(8, 272, 128), shape(128, 256)),
        in_specs=[ANY, VMEM],
        out_specs=(VMEM, VMEM),
        scratch_shapes=[pltpu.VMEM((8, 176, 128), BF16), pltpu.SemaphoreType.DMA((1,))],
        compiler_params=PARAMS,
    )(got, right)


def update_kernel(got, left, params, out, ends, held, back, sems):
    wait = pull([got], [held], sems)
    wait()
    for half in range(2):
        for y in range(8):
            start = half * 128 + y * 16
            rows = held[:, start : start + 16, :].reshape(128, 128)
            back[y * 128 : y * 128 + 128, half * 128 : half * 128 + 128] = rows
    moved = jnp.dot(left[...], back[...], preferred_element_type=F32)
    new = params[...].astype(F32) * (1.0 - 0.05 * 0.1) - 0.05 * moved
    new = new.astype(BF16).reshape(8, 16, 256)
    for copy in range(8):
        out[copy] = new
    out[lax.axis_index("rep")] = moved.astype(BF16).reshape(8, 16, 256)
    for layer, (low, high) in enumerate(ends_of(held[:, 256:272, :])):
        ends[0, layer] = jnp.broadcast_to(low, (8, 128))
        ends[1, layer] = jnp.broadcast_to(high, (8, 128))


def update_part(got, left, params):
    return pl.pallas_call(
        update_kernel,
        out_shape=(shape(8, 8, 16, 256), shape(2, 2, 8, 128, of=F32)),
        in_specs=[ANY, VMEM, VMEM],
        out_specs=(VMEM, VMEM),
        scratch_shapes=[
            pltpu.VMEM((8, 272, 128), BF16),
            pltpu.VMEM((1024, 256), BF16),
            pltpu.SemaphoreType.DMA((1,)),
        ],
        compiler_params=PARAMS,
    )(got, left, params)


def step_kernel(got, params, second, ends, params_new, update, levels, low_new, span_new, held, sems):
    rep = lax.axis_index("rep")
    wait = pull([got], [held], sems)
    wait()
    for panel in range(4):
        for block in range(8):
            start = block * 1024 + panel * 256
            params_new[:, :, start : start + 256] = held[block, panel]
    for panel in range(4):
        lanes = slice(panel * 256, panel * 256 + 256)
        change = held[rep, panel].astype(F32)
        update[:, :, lanes] = change
        new = params[:, :, lanes].astype(F32) * (1.0 - 0.05 * 0.1) - 0.05 * change
        own = pl.ds(pl.multiple_of(rep * 1024 + panel * 256, 256), 256)
        params_new[:, :, own] = new.astype(BF16)
    row = lax.broadcasted_iota(jnp.int32, (8, 128), 0)
    lane = lax.broadcasted_iota(jnp.int32, (8, 128), 1)
    for layer in range(2):
        low = ends[0, layer]
        span = ends[1, layer] - low
        for out, values in ((low_new, low), (span_new, span)):
            spread = jnp.sum(jnp.where(row == lane, values, 0.0), axis=0, keepdims=True)
            out[layer : layer + 1, :] = spread[:, 0:8]
        for group in range(8):
            lanes = slice(group * 128, group * 128 + 128)
            above = second[layer, :, lanes] - low[group : group + 1]
            levels[layer, :, lanes] = 15.0 * above / span[group : group + 1]


def step(got, params, second, ends):
    return pl.pallas_call(
        step_kernel,
        out_shape=(
            shape(2, 16, 8192),
            shape(2, 16, 1024, of=F32),
            shape(2, 16, 1024, of=F32),
            shape(2, 8, of=F32),
            shape(2, 8, of=F32),
        ),
        in_specs=[ANY, VMEM, VMEM, VMEM],
        out_specs=(VMEM,) * 5,
        scratch_shapes=[pltpu.VMEM((8, 4, 2, 16, 256), BF16), pltpu.SemaphoreType.DMA((1,))],
        compiler_params=PARAMS,
    )(got, params, second, ends)


def on_device(grads, params, left_basis, right_basis, moment, codes, level_low, level_span):
    odd = lax.axis_index("odd")
    flip = lambda values, axis, size, bit: lax.ppermute(values, axis, [(i, i ^ bit) for i in range(size)])
    tie = lax.optimization_barrier

    near = flip(right_basis, "core", 2, 1)
    near = jnp.where(
        lax.axis_index("core") == 0, jnp.stack([right_basis, near]), jnp.stack([near, right_basis])
    )
    rights = [near] + [flip(near, "x", 4, bits) for bits in (1, 2, 3)]

    sent = panels(grads[0], left_basis)
    got = exchange(sent.reshape(64, 16, 384), ZB)
    got, rights = tie((got, rights))
    part, left_rows, spread = left_part(got.reshape(8, 128, 384), level_low, level_span)

    layer = lambda values: lax.dynamic_index_in_dim(values, 1 - odd, 1, keepdims=False)
    other = flip(jnp.stack([layer(values) for values in rights]), "odd", 2, 1)

    got = exchange(part, A)
    turned, right_rows = right_part(got, rights, other)
    got = exchange(turned.reshape(8, 16, 1024), B).reshape(4, 2, 16, 1024)
    block, moment_new, second_new = moments(got, moment, codes, spread, params)
    got = exchange(block.reshape(8, 176, 128), B)
    block, old = back_part(got, right_rows.reshape(256, 1024))
    got = exchange(block, A)
    moved, ends = update_part(got, left_rows, old)
    got = exchange(moved.reshape(64, 16, 256), ZB).reshape(8, 4, 2, 16, 256)

    params_new, update, levels, low_new, span_new = step(got, params, second_new, ends)
    return (params_new, moment_new, update, levels, low_new, span_new)


def solution(mesh):
    fine = Mesh(mesh.devices.reshape(8, 4, 2, 4, 2), ("rep",) + F)
    return jax.shard_map(
        on_device,
        mesh=fine,
        in_specs=(
            P("rep", None, F, None),
            P(None, F, "rep"),
            P(None, F, None),
            P(None, ("rep",) + F, None),
            P(None, F, "rep"),
            P(None, F, "rep"),
            P(None, "rep"),
            P(None, "rep"),
        ),
        out_specs=(
            P(None, F, None),
            P(None, F, "rep"),
            P(None, F, "rep"),
            P(None, F, "rep"),
            P(None, "rep"),
            P(None, "rep"),
        ),
        check_vma=False,
    )
```
